32 devices in a mesh: swath: 16 (over z, x, core), chan: 2 (over y).
Axes of the slice: x: 2, y: 2, z: 4, core: 2. Of those that a mesh axis runs over, the one named last changes fastest.
Arguments:
- grid_profiles: bfloat16 [16384, 256], P('swath'), may hold values from -6 to 6
- send_lists: int32 [16, 16, 256], P('swath'), may hold values from 0 to 1023
- counts: int32 [16, 16], P('swath'), may hold values from 1 to 256, as said below
- angle_index: int32 [128], replicated, may hold values from 0 to 7
- jacobian: bfloat16 [3, 256, 608], P(None, None, 'chan'), may hold values from -0.375 to 0.375
- observed: bfloat16 [608, 65536], P('chan', 'swath'), may hold values from -6 to 6
- kappa: float32 [2, 608], P(None, 'chan'), may hold values from 0.04 to 0.24
- factor: bfloat16 [608, 608], P('chan')
Outputs:
- weighted: float32 [608, 65536], P('chan', 'swath')
The draws below stay inside these ranges and needn't reach their ends.
Inputs may be any that keep to these rules, and one draw needn't show every extreme that they name: `counts`: some receiver gets 256 live slots from every sender; every entry is at least one.
All inputs are finite; a program needn't handle non-finite values.
Results may differ from the reference program's by a relative error of at most 0.0029.
Values may be sent and summed in bfloat16 or wider, within the bound.
No kernel may reach another device: no remote copies, remote signals or barrier semaphores. Data moves between devices by JAX's collectives and lax.ppermute only.
A program may use at most 128 MiB of HBM per device.

```python
import math
import jax
import jax.numpy as jnp

CHAN = 608
PROF = 256
XTRACK = 128
NANG = 8
GROWS_DEV = 1024
CAP = 256
NPIX = 65536
NLINES = 512
GROWS = 16384
N_SWATH = 16


def draw_counts(key, part):
    first_key, second_key = jax.random.split(key)
    order = jax.random.permutation(first_key, N_SWATH)
    full_receiver = order < max(1, N_SWATH // 4)
    lowest = max(1, CAP // 6)
    highest = max(lowest + 1, CAP // 2 + 1)
    random_counts = jax.random.randint(second_key, (N_SWATH, N_SWATH), lowest, highest)
    return jnp.where(full_receiver[None, :], CAP, random_counts).astype(jnp.int32)


def draw_factor(key, part):
    first_key, second_key = jax.random.split(key)
    row_index = jnp.arange(CHAN)[:, None]
    col_index = jnp.arange(CHAN)[None, :]
    noise = jax.random.normal(first_key, (CHAN, CHAN), jnp.float32)
    lower = noise * 0.8 / jnp.sqrt((row_index + 1).astype(jnp.float32))
    diagonal = jnp.exp(jax.random.uniform(second_key, (CHAN,), jnp.float32, -0.5, 0.5))
    matrix = jnp.where(row_index > col_index, lower, 0.0)
    matrix = jnp.where(row_index == col_index, diagonal[:, None], matrix)
    return matrix.astype(jnp.bfloat16)


def touch_ends(drawn, key, smallest, largest):
    dims = drawn.shape
    index_at = [jax.random.randint(jax.random.fold_in(key, axis), (), 0, dims[axis]) for axis in range(len(dims))]
    drawn = drawn.at[tuple(index_at)].set(smallest)
    longest = dims.index(max(dims))
    index_at[longest] = (index_at[longest] + 1) % dims[longest]
    return drawn.at[tuple(index_at)].set(largest)


def shard_levels(stream_key, extent, cuts, low, largest):
    factor_of, own = 1.0, jax.random.fold_in(stream_key, 6)
    for position, parts in cuts:
        heights = jnp.exp(jax.random.uniform(jax.random.fold_in(own, position), (parts,), jnp.float32, low / len(cuts), largest / len(cuts)))
        factor_of = factor_of * jnp.repeat(heights, extent[position] // parts).reshape([-1 if axis == position else 1 for axis in range(len(extent))])
    return factor_of


def scatter_about(rng, extent, scale, limit, pieces=(), held_as=jnp.bfloat16):
    drawn = jax.random.normal(rng, extent, jnp.float32) * scale
    if len(pieces) > 0:
        drawn = shard_levels(rng, extent, pieces, -0.22, 0.18) * drawn
    return jnp.clip(drawn, min=-limit, max=limit).astype(held_as)


def setup_inputs(seed: int = 0) -> dict:
    key_of = jax.random.split(jax.random.key(seed), 9)
    return {
        "grid_profiles": scatter_about(key_of[0], (GROWS, PROF), 1.0, 6.0, ((0, 16),)),
        "send_lists": touch_ends(jax.random.randint(key_of[1], (N_SWATH, N_SWATH, CAP), 0, GROWS_DEV), jax.random.fold_in(key_of[1], 1), 0, GROWS_DEV - 1).astype(jnp.int32),
        "counts": draw_counts(jax.random.fold_in(key_of[8], 71), 0),
        "angle_index": touch_ends(jax.random.randint(key_of[3], (XTRACK,), 0, NANG), jax.random.fold_in(key_of[3], 1), 0, NANG - 1).astype(jnp.int32),
        "jacobian": scatter_about(key_of[4], (3, PROF, CHAN), PROF ** -0.5, 0.375, ((2, 2),)),
        "observed": scatter_about(key_of[5], (CHAN, NPIX), 1.0, 6.0, ((0, 2), (1, 16))),
        "kappa": jnp.clip(jnp.exp(math.log(0.24) - 1.7917595 * jax.random.uniform(key_of[6], (2, CHAN), jnp.float32) ** shard_levels(key_of[6], (2, CHAN), ((1, 2),), -0.2, 0.2)), 0.04, 0.24),
        "factor": draw_factor(jax.random.fold_in(key_of[8], 71), 0),
    }


max_zenith = math.pi / 3.0


def fetch_rows(grid_block, row_picks):
    return grid_block[row_picks]


def reference(grid_profiles, send_lists, counts, angle_index, jacobian, observed, kappa, factor):
    grid_r = grid_profiles.reshape(N_SWATH, GROWS_DEV, PROF)
    fetched = jax.vmap(fetch_rows)(grid_r, send_lists)
    live_slot = jnp.arange(CAP, dtype=jnp.int32)[None, None, :] < counts[:, :, None]
    fetched = jnp.where(live_slot[..., None], fetched, jnp.zeros((), fetched.dtype))
    pixel_profiles = fetched.transpose(1, 0, 2, 3).reshape(NPIX, PROF)
    column_bin = angle_index[jnp.arange(NPIX, dtype=jnp.int32) % XTRACK]
    slant_path = 1.0 / jnp.cos(column_bin.astype(jnp.float32) * (max_zenith / (NANG - 1))) - 1.0
    model_terms = [jnp.dot(jacobian[m].T, pixel_profiles.T, preferred_element_type=jnp.float32) for m in range(3)]
    slant_row = slant_path[None, :]
    departure = observed.astype(jnp.float32) - (model_terms[0] + slant_row * model_terms[1] + slant_row * slant_row * model_terms[2])
    smooth_field = departure.reshape(CHAN, NLINES, XTRACK)
    along_rate = kappa[0][:, None, None]
    cross_rate = kappa[1][:, None, None]
    for sweep in range(3):
        padded = jnp.pad(smooth_field, ((0, 0), (1, 1), (1, 1)))
        along_sum = padded[:, 2:, 1:-1] + padded[:, :-2, 1:-1] - 2.0 * smooth_field
        cross_sum = padded[:, 1:-1, 2:] + padded[:, 1:-1, :-2] - 2.0 * smooth_field
        smooth_field = smooth_field + along_rate * along_sum + cross_rate * cross_sum
    smoothed = smooth_field.reshape(CHAN, NPIX).astype(jnp.bfloat16)
    return jnp.dot(factor, smoothed, preferred_element_type=jnp.float32)
```

```python
import functools
import math

import jax
import jax.numpy as jnp
from jax import lax
from jax.experimental import pallas as pl
from jax.experimental.pallas import tpu as pltpu
from jax.sharding import PartitionSpec as P

XTRACK = 128
NANG = 8
HALO = 3
VMEM_LIMIT = 60 * 1024 * 1024


max_zenith = math.pi / 3.0


def extended_2(block, sides, width):
    for axis, dim in sides:
        count = lax.axis_size(axis)
        forward = [(i, i + 1) for i in range(count - 1)]
        backward = [(target, source) for source, target in forward]
        low = lax.ppermute(
            lax.slice_in_dim(block, block.shape[dim] - width, None, axis=dim), axis, forward
        )
        high = lax.ppermute(lax.slice_in_dim(block, 0, width, axis=dim), axis, backward)
        block = jnp.concatenate([low, block, high], axis=dim)
    return block


def diffuse_once(extended, along_rate, cross_rate):
    center = extended[:, 1:-1]
    along_sum = extended[:, 2:] + extended[:, :-2] - 2.0 * center
    side_pad = jnp.pad(center, ((0, 0), (0, 0), (1, 1)))
    cross_sum = side_pad[:, :, 2:] + side_pad[:, :, :-2] - 2.0 * center
    return center + along_rate * along_sum + cross_rate * cross_sum


def line_rims(smooth_field):
    return extended_2(smooth_field, (("swath", 1),), 1)


def slant_of(angle_index):
    zenith = angle_index.astype(jnp.float32) * (max_zenith / (NANG - 1))
    return 1.0 / jnp.cos(zenith) - 1.0


def on_device_plain(grid_profiles, send_lists, counts, angle_index, jacobian, observed, kappa, factor):
    slot_rows = send_lists[0]
    slots = slot_rows.shape[1]
    own_chan = observed.shape[0]
    pixel_count = observed.shape[1]
    line_count = pixel_count // XTRACK
    live_slot = jnp.arange(slots, dtype=jnp.int32)[None, :] < counts[0][:, None]
    zero_value = jnp.zeros((), grid_profiles.dtype)
    outgoing = jnp.where(live_slot[:, :, None], grid_profiles[slot_rows], zero_value)
    incoming = lax.all_to_all(outgoing, "swath", split_axis=0, concat_axis=0, tiled=True)
    pixel_profiles = incoming.reshape(pixel_count, grid_profiles.shape[1])
    model = jnp.einsum("mkc,pk->mcp", jacobian, pixel_profiles, preferred_element_type=jnp.float32)
    slant_path = slant_of(angle_index)
    model = model.reshape(3, own_chan, line_count, XTRACK)
    departure = observed.astype(jnp.float32).reshape(own_chan, line_count, XTRACK) - (
        model[0] + slant_path * model[1] + slant_path * slant_path * model[2]
    )
    along_rate = kappa[0][:, None, None]
    cross_rate = kappa[1][:, None, None]
    smooth_field = departure
    for sweep in range(3):
        smooth_field = diffuse_once(line_rims(smooth_field), along_rate, cross_rate)
    smoothed = smooth_field.reshape(own_chan, pixel_count).astype(jnp.bfloat16)
    return jnp.dot(
        factor,
        lax.all_gather(smoothed, "chan", axis=0, tiled=True),
        preferred_element_type=jnp.float32,
    )


def gather_kernel(idx_ref, grid_ref, out_ref):
    grid_rows = grid_ref.shape[0]
    slots, parts = idx_ref.shape
    row_number = lax.broadcasted_iota(jnp.int32, (slots, grid_rows), 1)
    for part in range(parts):
        one_hot = (idx_ref[:, part : part + 1] == row_number).astype(jnp.float32).astype(jnp.bfloat16)
        rows = jnp.dot(one_hot, grid_ref[...], preferred_element_type=jnp.float32)
        out_ref[part] = rows.astype(out_ref.dtype)


def gather_rows(grid_profiles, slot_rows, counts):
    parts, slots = slot_rows.shape
    live_slot = jnp.arange(slots, dtype=jnp.int32)[None, :] < counts[:, None]
    picks = jnp.where(live_slot, slot_rows, -1).T
    return pl.pallas_call(
        gather_kernel,
        out_shape=jax.ShapeDtypeStruct((parts, slots, grid_profiles.shape[1]), grid_profiles.dtype),
        compiler_params=pltpu.CompilerParams(vmem_limit_bytes=VMEM_LIMIT),
        name="pick_rows",
    )(picks, grid_profiles)


def main_kernel(
    prof_ref, prof_top_ref, prof_bot_ref,
    jac_own_ref, jac_oth_ref,
    obs_ref, mid_ref, bnd_ref, top_ref, bot_ref,
    rates_ref, rows_ref, factor_ref,
    out_ref,
    dep, smooth,
):
    own = obs_ref.shape[0]
    pixels = obs_ref.shape[1]
    rim = top_ref.shape[1]
    chans = 2 * own
    lines = pixels // XTRACK
    s1 = rows_ref[0:1, :]
    s2 = rows_ref[1:2, :]

    def model(jac, prof, obs, width):
        terms = [
            lax.dot_general(
                jac[m], prof, (((1,), (1,)), ((), ())), preferred_element_type=jnp.float32
            )
            for m in range(3)
        ]
        t1 = jnp.concatenate([s1] * (width // XTRACK), axis=1)
        t2 = jnp.concatenate([s2] * (width // XTRACK), axis=1)
        return obs.astype(jnp.float32) - (terms[0] + t1 * terms[1] + t2 * terms[2])

    for part, jac in enumerate((jac_own_ref, jac_oth_ref)):
        chan = slice(part * own, (part + 1) * own)
        dep[chan, 0:rim] = model(jac, prof_top_ref[...], top_ref[chan, :], rim)
        dep[chan, rim + pixels : pixels + 2 * rim] = model(jac, prof_bot_ref[...], bot_ref[chan, :], rim)

    wide = 2 * XTRACK

    def own_block(t, carry):
        at = pl.multiple_of(t * wide, wide)
        dep[0:own, pl.ds(pl.multiple_of(rim + at, XTRACK), wide)] = model(
            jac_own_ref, prof_ref[pl.ds(at, wide), :], obs_ref[:, pl.ds(at, wide)], wide
        )
        return carry

    lax.fori_loop(0, pixels // wide, own_block, 0)

    dep[own:chans, rim : 2 * rim] = model(jac_oth_ref, prof_ref[0:rim, :], bnd_ref[:, 0:rim], rim)
    dep[own:chans, pixels : pixels + rim] = model(
        jac_oth_ref, prof_ref[pixels - rim : pixels, :], bnd_ref[:, rim : 2 * rim], rim
    )

    def other_block(t, carry):
        at = pl.multiple_of(t * wide, wide)
        dep[own:chans, pl.ds(pl.multiple_of(2 * rim + at, XTRACK), wide)] = model(
            jac_oth_ref, prof_ref[pl.ds(pl.multiple_of(rim + at, XTRACK), wide), :],
            mid_ref[:, pl.ds(at, wide)], wide
        )
        return carry

    lax.fori_loop(0, (pixels - 2 * rim) // wide, other_block, 0)

    inside_top = rows_ref[2:3, :]
    inside_bot = rows_ref[3:4, :]
    total = lines + 2 * HALO

    def diffuse(i, carry):
        chan = pl.ds(pl.multiple_of(i * 16, 16), 16)
        along = rates_ref[0, chan, :]
        left = rates_ref[1, chan, :]
        right = rates_ref[2, chan, :]
        stay = rates_ref[3, chan, :]

        def sweep(before, here, after):
            return (
                stay * here
                + along * (before + after)
                + left * pltpu.roll(here, 1, 1)
                + right * pltpu.roll(here, XTRACK - 1, 1)
            )

        fields = [{}, {}, {}, {}]
        for j in range(total):
            fields[0][j] = dep[chan, j * XTRACK : (j + 1) * XTRACK]
            for k in range(1, HALO + 1):
                at = j - k
                if at < k:
                    continue
                prev = fields[k - 1]
                new = sweep(prev[at - 1], prev[at], prev[at + 1])
                if at < HALO:
                    new = new * inside_top
                if at >= HALO + lines:
                    new = new * inside_bot
                fields[k][at] = new
                del prev[at - 1]
                if k == HALO:
                    line = at - HALO
                    smooth[chan, line * XTRACK : (line + 1) * XTRACK] = new.astype(smooth.dtype)
        return carry

    lax.fori_loop(0, chans // 16, diffuse, 0)

    def factor_block(t, carry):
        at = pl.multiple_of(t * wide, wide)
        out_ref[:, pl.ds(at, wide)] = jnp.dot(
            factor_ref[...], smooth[:, pl.ds(at, wide)], preferred_element_type=jnp.float32
        )
        return carry

    lax.fori_loop(0, pixels // wide, factor_block, 0)


def on_device_two(grid_profiles, send_lists, counts, angle_index, jacobian, observed, kappa, factor):
    own, pixels = observed.shape
    rim = HALO * XTRACK
    swath = lax.axis_size("swath")
    place = lax.axis_index("swath")
    half = lax.axis_index("chan")
    swap = [(0, 1), (1, 0)]
    forward = [(i, i + 1) for i in range(swath - 1)]
    backward = [(i + 1, i) for i in range(swath - 1)]

    jac_own = jnp.swapaxes(jacobian, 1, 2)
    jac_oth = lax.ppermute(jac_own, "chan", swap)
    bnd_own = jnp.concatenate([observed[:, :rim], observed[:, pixels - rim :]], axis=1)
    bnd_oth = lax.ppermute(bnd_own, "chan", swap)
    mid_oth = lax.ppermute(observed[:, rim : pixels - rim], "chan", swap)
    kappa_oth = lax.ppermute(kappa, "chan", swap)

    outgoing = gather_rows(grid_profiles, send_lists[0], counts[0])
    incoming = lax.all_to_all(outgoing, "swath", split_axis=0, concat_axis=0, tiled=True)
    profiles = incoming.reshape(pixels, grid_profiles.shape[1])
    prof_top = lax.ppermute(profiles[pixels - rim :], "swath", forward)
    prof_bot = lax.ppermute(profiles[:rim], "swath", backward)

    both = jnp.concatenate([bnd_own, bnd_oth], axis=0)
    obs_top = lax.ppermute(both[:, rim:], "swath", forward)
    obs_bot = lax.ppermute(both[:, :rim], "swath", backward)

    rate = jnp.concatenate([kappa, kappa_oth], axis=1)[:, :, None]
    lane = jnp.arange(XTRACK, dtype=jnp.int32)[None, :]
    along, cross = rate[0], rate[1]
    ones = jnp.ones((1, XTRACK), jnp.float32)
    rates = jnp.stack([
        along * ones,
        cross * (lane > 0),
        cross * (lane < XTRACK - 1),
        (1.0 - 2.0 * along - 2.0 * cross) * ones,
    ])
    slant = slant_of(angle_index)
    rows = jnp.stack([
        slant,
        slant * slant,
        jnp.where(place > 0, ones[0], 0.0),
        jnp.where(place < swath - 1, ones[0], 0.0),
    ])
    factor_two = jnp.where(half == 0, factor, jnp.roll(factor, own, axis=1))

    return pl.pallas_call(
        main_kernel,
        out_shape=jax.ShapeDtypeStruct((own, pixels), jnp.float32),
        scratch_shapes=[
            pltpu.VMEM((2 * own, pixels + 2 * rim), jnp.float32),
            pltpu.VMEM((2 * own, pixels), jnp.bfloat16),
        ],
        compiler_params=pltpu.CompilerParams(vmem_limit_bytes=VMEM_LIMIT),
        name="departures_sweeps_factor",
    )(
        profiles, prof_top, prof_bot, jac_own, jac_oth,
        observed, mid_oth, bnd_oth, obs_top, obs_bot,
        rates, rows, factor_two,
    )


def solution(mesh):
    in_specs = (
        P("swath", None),
        P("swath", None, None),
        P("swath", None),
        P(),
        P(None, None, "chan"),
        P("chan", "swath"),
        P(None, "chan"),
        P("chan", None),
    )
    out_specs = P("chan", "swath")
    on_device = on_device_two if mesh.shape["chan"] == 2 else on_device_plain
    return jax.shard_map(
        on_device, mesh=mesh, in_specs=in_specs, out_specs=out_specs, check_vma=False
    )
```

```python
import functools
import math

import jax
import jax.numpy as jnp
import numpy as np
from jax import lax
from jax.experimental import pallas as pl
from jax.experimental.pallas import tpu as pltpu
from jax.sharding import PartitionSpec as P

XTRACK = 128
NANG = 8
HALO = 3
OUT_BLOCK = 1024
VMEM_LIMIT = 60 * 1024 * 1024


max_zenith = math.pi / 3.0


def extended_2(block, sides, width):
    for axis, dim in sides:
        count = lax.axis_size(axis)
        forward = [(i, i + 1) for i in range(count - 1)]
        backward = [(target, source) for source, target in forward]
        low = lax.ppermute(
            lax.slice_in_dim(block, block.shape[dim] - width, None, axis=dim), axis, forward
        )
        high = lax.ppermute(lax.slice_in_dim(block, 0, width, axis=dim), axis, backward)
        block = jnp.concatenate([low, block, high], axis=dim)
    return block


def diffuse_once(extended, along_rate, cross_rate):
    center = extended[:, 1:-1]
    along_sum = extended[:, 2:] + extended[:, :-2] - 2.0 * center
    side_pad = jnp.pad(center, ((0, 0), (0, 0), (1, 1)))
    cross_sum = side_pad[:, :, 2:] + side_pad[:, :, :-2] - 2.0 * center
    return center + along_rate * along_sum + cross_rate * cross_sum


def line_rims(smooth_field):
    return extended_2(smooth_field, (("swath", 1),), 1)


def slant_of(angle_index):
    zenith = angle_index.astype(jnp.float32) * (max_zenith / (NANG - 1))
    return 1.0 / jnp.cos(zenith) - 1.0


def on_device_plain(grid_profiles, send_lists, counts, angle_index, jacobian, observed, kappa, factor):
    slot_rows = send_lists[0]
    slots = slot_rows.shape[1]
    own_chan = observed.shape[0]
    pixel_count = observed.shape[1]
    line_count = pixel_count // XTRACK
    live_slot = jnp.arange(slots, dtype=jnp.int32)[None, :] < counts[0][:, None]
    zero_value = jnp.zeros((), grid_profiles.dtype)
    outgoing = jnp.where(live_slot[:, :, None], grid_profiles[slot_rows], zero_value)
    incoming = lax.all_to_all(outgoing, "swath", split_axis=0, concat_axis=0, tiled=True)
    pixel_profiles = incoming.reshape(pixel_count, grid_profiles.shape[1])
    model = jnp.einsum("mkc,pk->mcp", jacobian, pixel_profiles, preferred_element_type=jnp.float32)
    slant_path = slant_of(angle_index)
    model = model.reshape(3, own_chan, line_count, XTRACK)
    departure = observed.astype(jnp.float32).reshape(own_chan, line_count, XTRACK) - (
        model[0] + slant_path * model[1] + slant_path * slant_path * model[2]
    )
    along_rate = kappa[0][:, None, None]
    cross_rate = kappa[1][:, None, None]
    smooth_field = departure
    for sweep in range(3):
        smooth_field = diffuse_once(line_rims(smooth_field), along_rate, cross_rate)
    smoothed = smooth_field.reshape(own_chan, pixel_count).astype(jnp.bfloat16)
    return jnp.dot(
        factor,
        lax.all_gather(smoothed, "chan", axis=0, tiled=True),
        preferred_element_type=jnp.float32,
    )


def gather_kernel(idx_ref, grid_ref, out_ref):
    grid_rows = grid_ref.shape[0]
    slots, parts = idx_ref.shape
    row_number = lax.broadcasted_iota(jnp.int32, (slots, grid_rows), 1)
    for part in range(parts):
        one_hot = (idx_ref[:, part : part + 1] == row_number).astype(jnp.float32).astype(jnp.bfloat16)
        rows = jnp.dot(one_hot, grid_ref[...], preferred_element_type=jnp.float32)
        out_ref[part] = rows.astype(out_ref.dtype)


def gather_rows(grid_profiles, slot_rows, counts):
    parts, slots = slot_rows.shape
    live_slot = jnp.arange(slots, dtype=jnp.int32)[None, :] < counts[:, None]
    picks = jnp.where(live_slot, slot_rows, -1).T
    return pl.pallas_call(
        gather_kernel,
        out_shape=jax.ShapeDtypeStruct((parts, slots, grid_profiles.shape[1]), grid_profiles.dtype),
        compiler_params=pltpu.CompilerParams(vmem_limit_bytes=VMEM_LIMIT),
        name="pick_rows",
    )(picks, grid_profiles)


def main_kernel(
    prof_hbm, prof_top_hbm, prof_bot_hbm, obs_hbm, mid_hbm, bnd_hbm, top_hbm, bot_hbm,
    jac_own_ref, jac_oth_ref, rates_ref, rows_ref, shift_ref, factor_ref,
    out_hbm,
    prof, obs, field, smooth, out, sems, out_sems,
):
    own, pixels = obs_hbm.shape
    rim = top_hbm.shape[1]
    lines = pixels // XTRACK
    wide = 2 * XTRACK
    full = pixels + 2 * rim
    mine, theirs = pl.ds(0, own), pl.ds(own, own)
    copies = [
        (prof_hbm, prof.at[pl.ds(rim, pixels), :]),
        (prof_top_hbm, prof.at[pl.ds(0, rim), :]),
        (prof_bot_hbm, prof.at[pl.ds(rim + pixels, rim), :]),
        (obs_hbm, obs.at[mine, pl.ds(rim, pixels)]),
        (top_hbm, obs.at[:, pl.ds(0, rim)]),
        (bot_hbm, obs.at[:, pl.ds(rim + pixels, rim)]),
        (mid_hbm, obs.at[theirs, pl.ds(2 * rim, pixels - 2 * rim)]),
        (bnd_hbm.at[:, pl.ds(0, rim)], obs.at[theirs, pl.ds(rim, rim)]),
        (bnd_hbm.at[:, pl.ds(rim, rim)], obs.at[theirs, pl.ds(pixels, rim)]),
    ]
    copies = [pltpu.make_async_copy(src, dst, sems.at[n]) for n, (src, dst) in enumerate(copies)]
    for copy in copies:
        copy.start()
    s1 = jnp.concatenate([rows_ref[0:1, :]] * 2, axis=1)
    s2 = jnp.concatenate([rows_ref[1:2, :]] * 2, axis=1)
    inside_top = rows_ref[2:3, :]
    inside_bot = rows_ref[3:4, :]
    shift = shift_ref[...]

    def departures(part, jac, t):
        at = pl.multiple_of(t * wide, wide)
        here = prof[pl.ds(at, wide), :]
        terms = [
            lax.dot_general(jac[m], here, (((1,), (1,)), ((), ())), preferred_element_type=jnp.float32)
            for m in range(3)
        ]
        dep = obs[pl.ds(part * own, own), pl.ds(at, wide)].astype(jnp.float32) - (
            terms[0] + s1 * terms[1] + s2 * terms[2]
        )
        field[0, :, pl.ds(at, wide)] = dep
        high = dep.astype(jnp.bfloat16)
        low = (dep - high.astype(jnp.float32)).astype(jnp.bfloat16)
        for n in range(2):
            lanes = slice(n * XTRACK, (n + 1) * XTRACK)
            pair = jnp.concatenate([high[:, lanes], low[:, lanes]], axis=1)
            moved = jnp.dot(pair, shift, preferred_element_type=jnp.float32)
            for k in range(HALO):
                field[k + 1, :, pl.ds(pl.multiple_of(at + n * XTRACK, XTRACK), XTRACK)] = moved[
                    :, k * XTRACK : (k + 1) * XTRACK
                ]

    def sweeps(part, i):
        rows = pl.ds(pl.multiple_of(i * 16, 16), 16)
        chan = pl.ds(pl.multiple_of(part * own + i * 16, 16), 16)
        stay, along = rates_ref[0, chan, :], rates_ref[1, chan, :]
        cross = [rates_ref[2 + k, chan, :] for k in range(HALO)]
        fields = [{}, {}, {}, {}]
        for j in range(lines + 2 * HALO):
            fields[0][j] = field[0, rows, j * XTRACK : (j + 1) * XTRACK]
            for k in range(1, HALO + 1):
                at = j - k
                if at < k:
                    continue
                prev = fields[k - 1]
                new = (
                    stay * prev[at]
                    + along * (prev[at - 1] + prev[at + 1])
                    + cross[k - 1] * field[k, rows, at * XTRACK : (at + 1) * XTRACK]
                )
                if at < HALO:
                    new = new * inside_top
                if at >= HALO + lines:
                    new = new * inside_bot
                fields[k][at] = new
                del prev[at - 1]
                if k == HALO:
                    line = at - HALO
                    smooth[chan, line * XTRACK : (line + 1) * XTRACK] = new.astype(smooth.dtype)

    for part, jac in enumerate((jac_own_ref, jac_oth_ref)):
        for copy in copies[:6] if part == 0 else copies[6:]:
            copy.wait()
        pl.loop(0, full // wide, unroll=4)(functools.partial(departures, part, jac))
        pl.loop(0, own // 16)(functools.partial(sweeps, part))

    def out_copy(t):
        at = pl.multiple_of(t * OUT_BLOCK, OUT_BLOCK)
        return pltpu.make_async_copy(
            out.at[:, pl.ds(at, OUT_BLOCK)], out_hbm.at[:, pl.ds(at, OUT_BLOCK)], out_sems.at[t]
        )

    def weigh(t):
        at = pl.multiple_of(t * OUT_BLOCK, OUT_BLOCK)
        out[:, pl.ds(at, OUT_BLOCK)] = jnp.dot(
            factor_ref[...], smooth[:, pl.ds(at, OUT_BLOCK)], preferred_element_type=jnp.float32
        )
        out_copy(t).start()

    blocks = pixels // (OUT_BLOCK)
    pl.loop(0, blocks)(weigh)
    pl.loop(0, blocks)(lambda t: out_copy(t).wait())

def on_device_two(grid_profiles, send_lists, counts, angle_index, jacobian, observed, kappa, factor):
    own, pixels = observed.shape
    rim = HALO * XTRACK
    swath = lax.axis_size("swath")
    place = lax.axis_index("swath")
    half = lax.axis_index("chan")
    swap = [(0, 1), (1, 0)]
    forward = [(i, i + 1) for i in range(swath - 1)]
    backward = [(i + 1, i) for i in range(swath - 1)]

    bnd_own = jnp.concatenate([observed[:, :rim], observed[:, pixels - rim :]], axis=1)
    bnd_oth = lax.ppermute(bnd_own, "chan", swap)
    jac_own = jnp.swapaxes(jacobian, 1, 2)
    jac_half = lax.dynamic_slice_in_dim(jac_own, (place % 2) * (own // 2), own // 2, axis=1)
    jac_near = lax.ppermute(jac_half, "chan", swap)
    jac_far = lax.ppermute(jac_near, "swath", [(i, i ^ 1) for i in range(swath)])
    jac_oth = jnp.where(
        place % 2 == 0,
        jnp.concatenate([jac_near, jac_far], axis=1),
        jnp.concatenate([jac_far, jac_near], axis=1),
    )
    kappa_oth = lax.ppermute(kappa, "chan", swap)
    bnd_held, middle = lax.optimization_barrier((bnd_own, observed[:, rim : pixels - rim]))
    mid_oth = lax.ppermute(middle, "chan", swap)

    outgoing = gather_rows(grid_profiles, send_lists[0], counts[0])
    incoming = lax.all_to_all(outgoing, "swath", split_axis=0, concat_axis=0, tiled=True)
    profiles = incoming.reshape(pixels, grid_profiles.shape[1])
    prof_top = lax.ppermute(profiles[pixels - rim :], "swath", forward)
    prof_bot = lax.ppermute(profiles[:rim], "swath", backward)

    both = jnp.concatenate([bnd_held, bnd_oth], axis=0)
    obs_top = lax.ppermute(both[:, rim:], "swath", forward)
    obs_bot = lax.ppermute(both[:, :rim], "swath", backward)

    rate = jnp.concatenate([kappa, kappa_oth], axis=1)[:, :, None]
    along, cross = rate[0], rate[1]
    ones = jnp.ones((1, XTRACK), jnp.float32)
    rates = jnp.stack([
        (1.0 - 2.0 * along - 2.0 * cross) * ones,
        along * ones,
        3.0 * cross * ones,
        3.0 * cross * cross * ones,
        cross * cross * cross * ones,
    ])
    near = np.eye(XTRACK, k=1) + np.eye(XTRACK, k=-1)
    moves = np.concatenate([near, near @ near, near @ near @ near], axis=1)
    shift = jnp.asarray(np.concatenate([moves, moves], axis=0), jnp.bfloat16)
    slant = slant_of(angle_index)
    rows = jnp.stack([
        slant,
        slant * slant,
        jnp.where(place > 0, ones[0], 0.0),
        jnp.where(place < swath - 1, ones[0], 0.0),
    ])
    factor_two = jnp.where(half == 0, factor, jnp.roll(factor, own, axis=1))

    full = pixels + 2 * rim
    return pl.pallas_call(
        main_kernel,
        out_shape=jax.ShapeDtypeStruct((own, pixels), jnp.float32),
        in_specs=[pl.BlockSpec(memory_space=pl.ANY)] * 8 + [pl.BlockSpec(memory_space=pltpu.VMEM)] * 6,
        out_specs=pl.BlockSpec(memory_space=pl.ANY),
        scratch_shapes=[
            pltpu.VMEM((full, profiles.shape[1]), jnp.bfloat16),
            pltpu.VMEM((2 * own, full), jnp.bfloat16),
            pltpu.VMEM((HALO + 1, own, full), jnp.float32),
            pltpu.VMEM((2 * own, pixels), jnp.bfloat16),
            pltpu.VMEM((own, pixels), jnp.float32),
            pltpu.SemaphoreType.DMA((9,)),
            pltpu.SemaphoreType.DMA((pixels // OUT_BLOCK,)),
        ],
        compiler_params=pltpu.CompilerParams(vmem_limit_bytes=VMEM_LIMIT),
        name="departures_sweeps_factor",
    )(
        profiles, prof_top, prof_bot, observed, mid_oth, bnd_oth, obs_top, obs_bot,
        jac_own, jac_oth, rates, rows, shift, factor_two,
    )


def solution(mesh):
    in_specs = (
        P("swath", None),
        P("swath", None, None),
        P("swath", None),
        P(),
        P(None, None, "chan"),
        P("chan", "swath"),
        P(None, "chan"),
        P("chan", None),
    )
    out_specs = P("chan", "swath")
    on_device = on_device_two if mesh.shape["chan"] == 2 else on_device_plain
    return jax.shard_map(
        on_device, mesh=mesh, in_specs=in_specs, out_specs=out_specs, check_vma=False
    )
```

```python
import functools
import math

import jax
import jax.numpy as jnp
import numpy as np
from jax import lax
from jax.experimental import pallas as pl
from jax.experimental.pallas import tpu as pltpu
from jax.sharding import PartitionSpec as P

XTRACK = 128
NANG = 8
HALO = 3
OUT_BLOCK = 1024
GATHER_LIMIT = 24 * 1024 * 1024
VMEM_LIMIT = 60 * 1024 * 1024


max_zenith = math.pi / 3.0


def extended_2(block, sides, width):
    for axis, dim in sides:
        count = lax.axis_size(axis)
        forward = [(i, i + 1) for i in range(count - 1)]
        backward = [(target, source) for source, target in forward]
        low = lax.ppermute(
            lax.slice_in_dim(block, block.shape[dim] - width, None, axis=dim), axis, forward
        )
        high = lax.ppermute(lax.slice_in_dim(block, 0, width, axis=dim), axis, backward)
        block = jnp.concatenate([low, block, high], axis=dim)
    return block


def diffuse_once(extended, along_rate, cross_rate):
    center = extended[:, 1:-1]
    along_sum = extended[:, 2:] + extended[:, :-2] - 2.0 * center
    side_pad = jnp.pad(center, ((0, 0), (0, 0), (1, 1)))
    cross_sum = side_pad[:, :, 2:] + side_pad[:, :, :-2] - 2.0 * center
    return center + along_rate * along_sum + cross_rate * cross_sum


def line_rims(smooth_field):
    return extended_2(smooth_field, (("swath", 1),), 1)


def slant_of(angle_index):
    zenith = angle_index.astype(jnp.float32) * (max_zenith / (NANG - 1))
    return 1.0 / jnp.cos(zenith) - 1.0


def on_device_plain(grid_profiles, send_lists, counts, angle_index, jacobian, observed, kappa, factor):
    slot_rows = send_lists[0]
    slots = slot_rows.shape[1]
    own_chan = observed.shape[0]
    pixel_count = observed.shape[1]
    line_count = pixel_count // XTRACK
    live_slot = jnp.arange(slots, dtype=jnp.int32)[None, :] < counts[0][:, None]
    zero_value = jnp.zeros((), grid_profiles.dtype)
    outgoing = jnp.where(live_slot[:, :, None], grid_profiles[slot_rows], zero_value)
    incoming = lax.all_to_all(outgoing, "swath", split_axis=0, concat_axis=0, tiled=True)
    pixel_profiles = incoming.reshape(pixel_count, grid_profiles.shape[1])
    model = jnp.einsum("mkc,pk->mcp", jacobian, pixel_profiles, preferred_element_type=jnp.float32)
    slant_path = slant_of(angle_index)
    model = model.reshape(3, own_chan, line_count, XTRACK)
    departure = observed.astype(jnp.float32).reshape(own_chan, line_count, XTRACK) - (
        model[0] + slant_path * model[1] + slant_path * slant_path * model[2]
    )
    along_rate = kappa[0][:, None, None]
    cross_rate = kappa[1][:, None, None]
    smooth_field = departure
    for sweep in range(3):
        smooth_field = diffuse_once(line_rims(smooth_field), along_rate, cross_rate)
    smoothed = smooth_field.reshape(own_chan, pixel_count).astype(jnp.bfloat16)
    return jnp.dot(
        factor,
        lax.all_gather(smoothed, "chan", axis=0, tiled=True),
        preferred_element_type=jnp.float32,
    )


def gather_kernel(lists_ref, counts_ref, grid_ref, out_ref):
    grid_rows = grid_ref.shape[0]
    parts, slots = lists_ref.shape
    slot_number = lax.broadcasted_iota(jnp.int32, (slots, parts), 0)
    picks = jnp.where(slot_number < counts_ref[...], lists_ref[...].T, -1)
    row_number = lax.broadcasted_iota(jnp.int32, (slots, grid_rows), 1)
    for part in range(parts):
        one_hot = (picks[:, part : part + 1] == row_number).astype(jnp.float32).astype(jnp.bfloat16)
        rows = jnp.dot(one_hot, grid_ref[...], preferred_element_type=jnp.float32)
        out_ref[part] = rows.astype(out_ref.dtype)


def gather_rows(grid_profiles, slot_rows, counts):
    parts, slots = slot_rows.shape
    return pl.pallas_call(
        gather_kernel,
        out_shape=jax.ShapeDtypeStruct((parts, slots, grid_profiles.shape[1]), grid_profiles.dtype),
        compiler_params=pltpu.CompilerParams(vmem_limit_bytes=GATHER_LIMIT),
        name="pick_rows",
    )(slot_rows, counts, grid_profiles)


def half_kernel(last, *refs):
    prof_hbm, prof_top_hbm, prof_bot_hbm, top_hbm, bot_hbm = refs[:5]
    if last:
        mid_hbm, bnd_hbm, smooth_hbm, jac_ref, rates_ref, rows_ref, shift_ref, factor_ref = refs[5:13]
        out_hbm, prof, obs, field, moved_a, moved_b, sems, smooth, out, out_sems = refs[13:]
    else:
        obs_hbm, jac_ref, rates_ref, rows_ref, shift_ref = refs[5:10]
        smooth, prof, obs, field, moved_a, moved_b, sems = refs[10:]
    own, pixels = jac_ref.shape[1], prof_hbm.shape[0]
    rim = prof_top_hbm.shape[0]
    lines = pixels // XTRACK
    wide = 2 * XTRACK
    full = pixels + 2 * rim
    total = full // XTRACK
    first = own if last else 0

    part = pl.ds(first, own)
    copies = [
        (prof_top_hbm, prof.at[pl.ds(0, rim), :]),
        (top_hbm.at[part, :], obs.at[:, pl.ds(0, rim)]),
        (prof_hbm, prof.at[pl.ds(rim, pixels), :]),
        (prof_bot_hbm, prof.at[pl.ds(rim + pixels, rim), :]),
        (bot_hbm.at[part, :], obs.at[:, pl.ds(rim + pixels, rim)]),
    ]
    if last:
        copies += [
            (bnd_hbm.at[:, pl.ds(0, rim)], obs.at[:, pl.ds(rim, rim)]),
            (mid_hbm, obs.at[:, pl.ds(2 * rim, pixels - 2 * rim)]),
            (bnd_hbm.at[:, pl.ds(rim, rim)], obs.at[:, pl.ds(pixels, rim)]),
            (smooth_hbm, smooth.at[pl.ds(0, own), :]),
        ]
    else:
        copies.append((obs_hbm, obs.at[:, pl.ds(rim, pixels)]))
    copies = [pltpu.make_async_copy(src, dst, sems.at[n]) for n, (src, dst) in enumerate(copies)]
    for copy in copies:
        copy.start()
    s1 = jnp.concatenate([rows_ref[0:1, :]] * 2, axis=1)
    s2 = jnp.concatenate([rows_ref[1:2, :]] * 2, axis=1)
    inside_top = rows_ref[2:3, :]
    inside_bot = rows_ref[3:4, :]

    def departures(t):
        at = pl.multiple_of(t * wide, wide)
        here = prof[pl.ds(at, wide), :]
        terms = [
            lax.dot_general(jac_ref[m], here, (((1,), (1,)), ((), ())), preferred_element_type=jnp.float32)
            for m in range(3)
        ]
        field[:, pl.ds(at, wide)] = obs[:, pl.ds(at, wide)].astype(jnp.float32) - (
            terms[0] + s1 * terms[1] + s2 * terms[2]
        )

    def shifts(i, moved):
        rows = pl.ds(pl.multiple_of(i * 16, 16), 16)
        tiles = []
        for j in range(total):
            here = field[rows, j * XTRACK : (j + 1) * XTRACK]
            high = here.astype(jnp.bfloat16)
            low = (here - high.astype(jnp.float32)).astype(jnp.bfloat16)
            tiles.append(jnp.concatenate([high, low], axis=1))
        moved[...] = jnp.dot(
            jnp.concatenate(tiles, axis=0), shift_ref[...], preferred_element_type=jnp.float32
        )

    def sweeps(i, moved):
        rows = pl.ds(pl.multiple_of(i * 16, 16), 16)
        chan = pl.ds(pl.multiple_of(first + i * 16, 16), 16)
        along = jnp.broadcast_to(rates_ref[rows, 0:1], (16, XTRACK))
        cross = jnp.broadcast_to(rates_ref[rows, 1:2], (16, XTRACK))
        stay = 1.0 - 2.0 * along - 2.0 * cross
        cross = [3.0 * cross, 3.0 * cross * cross, cross * cross * cross]
        fields = [{}, {}, {}, {}]
        for j in range(total):
            fields[0][j] = field[rows, j * XTRACK : (j + 1) * XTRACK]
            for k in range(1, HALO + 1):
                at = j - k
                if at < k:
                    continue
                prev = fields[k - 1]
                new = (
                    stay * prev[at]
                    + along * (prev[at - 1] + prev[at + 1])
                    + cross[k - 1] * moved[at * 16 : (at + 1) * 16, (k - 1) * XTRACK : k * XTRACK]
                )
                if at < HALO:
                    new = new * inside_top
                if at >= HALO + lines:
                    new = new * inside_bot
                fields[k][at] = new
                del prev[at - 1]
                if k == HALO:
                    line = at - HALO
                    smooth[chan, line * XTRACK : (line + 1) * XTRACK] = new.astype(smooth.dtype)

    for copy in copies[:8]:
        copy.wait()
    pl.loop(0, total // 2, unroll=4)(departures)

    groups = own // 16
    shifts(0, moved_a)

    @pl.loop(0, groups // 2)
    def _(h):
        shifts(2 * h + 1, moved_b)
        sweeps(2 * h, moved_a)
        shifts(jnp.minimum(2 * h + 2, groups - 1), moved_a)
        sweeps(2 * h + 1, moved_b)

    if groups % 2:
        sweeps(groups - 1, moved_a)

    if not last:
        return
    copies[8].wait()

    def out_copy(t):
        at = pl.multiple_of(t * OUT_BLOCK, OUT_BLOCK)
        return pltpu.make_async_copy(
            out.at[:, pl.ds(at, OUT_BLOCK)], out_hbm.at[:, pl.ds(at, OUT_BLOCK)], out_sems.at[t]
        )

    @pl.loop(0, pixels // OUT_BLOCK)
    def _(t):
        at = pl.multiple_of(t * OUT_BLOCK, OUT_BLOCK)
        out[:, pl.ds(at, OUT_BLOCK)] = jnp.dot(
            factor_ref[...], smooth[:, pl.ds(at, OUT_BLOCK)], preferred_element_type=jnp.float32
        )
        out_copy(t).start()

    pl.loop(0, pixels // OUT_BLOCK)(lambda t: out_copy(t).wait())


def half_call(last, anys, whole):
    own, pixels = whole[0].shape[1], anys[0].shape[0]
    rim = anys[1].shape[0]
    full = pixels + 2 * rim
    scratch = [
        pltpu.VMEM((full, anys[0].shape[1]), jnp.bfloat16),
        pltpu.VMEM((own, full), jnp.bfloat16),
        pltpu.VMEM((own, full), jnp.float32),
        pltpu.VMEM((16 * (full // XTRACK), HALO * XTRACK), jnp.float32),
        pltpu.VMEM((16 * (full // XTRACK), HALO * XTRACK), jnp.float32),
        pltpu.SemaphoreType.DMA((9,)),
    ]
    if last:
        out_shape = jax.ShapeDtypeStruct((own, pixels), jnp.float32)
        out_spec = pl.BlockSpec(memory_space=pl.ANY)
        scratch += [
            pltpu.VMEM((2 * own, pixels), jnp.bfloat16),
            pltpu.VMEM((own, pixels), jnp.float32),
            pltpu.SemaphoreType.DMA((pixels // OUT_BLOCK,)),
        ]
    else:
        out_shape = jax.ShapeDtypeStruct((own, pixels), jnp.bfloat16)
        out_spec = pl.BlockSpec(memory_space=pltpu.VMEM)
    return pl.pallas_call(
        functools.partial(half_kernel, last),
        out_shape=out_shape,
        in_specs=[pl.BlockSpec(memory_space=pl.ANY)] * len(anys)
        + [pl.BlockSpec(memory_space=pltpu.VMEM)] * len(whole),
        out_specs=out_spec,
        scratch_shapes=scratch,
        compiler_params=pltpu.CompilerParams(vmem_limit_bytes=VMEM_LIMIT),
        cost_estimate=None if last else pl.CostEstimate(flops=1, bytes_accessed=1, transcendentals=0),
        name="other_half_and_factor" if last else "own_half",
    )(*anys, *whole)


def on_device_two(grid_profiles, send_lists, counts, angle_index, jacobian, observed, kappa, factor):
    own, pixels = observed.shape
    rim = HALO * XTRACK
    swath = lax.axis_size("swath")
    place = lax.axis_index("swath")
    half = lax.axis_index("chan")
    swap = [(0, 1), (1, 0)]
    forward = [(i, i + 1) for i in range(swath - 1)]
    backward = [(i + 1, i) for i in range(swath - 1)]

    def halos(block, axis):
        size = block.shape[axis]
        tail = lax.slice_in_dim(block, size - rim, size, axis=axis)
        head = lax.slice_in_dim(block, 0, rim, axis=axis)
        return lax.ppermute(tail, "swath", forward), lax.ppermute(head, "swath", backward)

    jac_own = jnp.swapaxes(jacobian, 1, 2)
    jac_half = lax.dynamic_slice_in_dim(jac_own, (place % 2) * (own // 2), own // 2, axis=1)
    jac_near = lax.ppermute(jac_half, "chan", swap)
    rates_own = kappa.T
    rates_oth = lax.ppermute(rates_own, "chan", swap)
    bnd_own = jnp.concatenate([observed[:, :rim], observed[:, pixels - rim :]], axis=1)
    bnd_oth = lax.ppermute(bnd_own, "chan", swap)
    outgoing = gather_rows(grid_profiles, send_lists[0], counts)
    outgoing, obs_late, bnd_own = lax.optimization_barrier((outgoing, observed, bnd_own))
    incoming = lax.all_to_all(outgoing, "swath", split_axis=0, concat_axis=0, tiled=True)
    middle = obs_late[:, rim : pixels - rim]
    middle, jac_near, bnd_oth = lax.optimization_barrier((middle, jac_near, bnd_oth))
    mid_oth = lax.ppermute(middle, "chan", swap)
    jac_far = lax.ppermute(jac_near, "swath", [(i, i ^ 1) for i in range(swath)])
    jac_oth = jnp.where(
        place % 2 == 0,
        jnp.concatenate([jac_near, jac_far], axis=1),
        jnp.concatenate([jac_far, jac_near], axis=1),
    )
    near = np.eye(XTRACK, k=1) + np.eye(XTRACK, k=-1)
    moves = np.concatenate([near, near @ near, near @ near @ near], axis=1)
    shift = jnp.asarray(np.concatenate([moves, moves], axis=0), jnp.bfloat16)
    slant = slant_of(angle_index)
    ones = jnp.ones((XTRACK,), jnp.float32)
    rows = jnp.stack([
        slant,
        slant * slant,
        jnp.where(place > 0, ones, 0.0),
        jnp.where(place < swath - 1, ones, 0.0),
    ])
    factor_two = jnp.where(half == 0, factor, jnp.roll(factor, own, axis=1))

    bnd_own, bnd_oth, jac_oth, rates_oth, rows, factor_two = lax.optimization_barrier(
        (bnd_own, bnd_oth, jac_oth, rates_oth, rows, factor_two)
    )
    bnd_both = jnp.concatenate([bnd_own, bnd_oth], axis=0)
    obs_top = lax.ppermute(bnd_both[:, rim:], "swath", forward)
    obs_bot = lax.ppermute(bnd_both[:, :rim], "swath", backward)

    profiles = incoming.reshape(pixels, grid_profiles.shape[1])
    prof_halos = halos(profiles, 0)

    smooth_own = half_call(
        False, (profiles, *prof_halos, obs_top, obs_bot, observed), (jac_own, rates_own, rows, shift)
    )
    return half_call(
        True,
        (profiles, *prof_halos, obs_top, obs_bot, mid_oth, bnd_oth, smooth_own),
        (jac_oth, rates_oth, rows, shift, factor_two),
    )


def solution(mesh):
    in_specs = (
        P("swath", None),
        P("swath", None, None),
        P("swath", None),
        P(),
        P(None, None, "chan"),
        P("chan", "swath"),
        P(None, "chan"),
        P("chan", None),
    )
    out_specs = P("chan", "swath")
    on_device = on_device_two if mesh.shape["chan"] == 2 else on_device_plain
    return jax.shard_map(
        on_device, mesh=mesh, in_specs=in_specs, out_specs=out_specs, check_vma=False
    )
```

```python
import functools
import math

import jax
import jax.numpy as jnp
import numpy as np
from jax import lax
from jax.experimental import pallas as pl
from jax.experimental.pallas import tpu as pltpu
from jax.sharding import PartitionSpec as P

XTRACK = 128
NANG = 8
HALO = 3
OUT_BLOCK = 512
GATHER_LIMIT = 24 * 1024 * 1024
OWN_LIMIT = 60 * 1024 * 1024
LAST_LIMIT = 60 * 1024 * 1024
SEGMENTS = 4
AHEAD = 2


max_zenith = math.pi / 3.0


def extended_2(block, sides, width):
    for axis, dim in sides:
        count = lax.axis_size(axis)
        forward = [(i, i + 1) for i in range(count - 1)]
        backward = [(target, source) for source, target in forward]
        low = lax.ppermute(
            lax.slice_in_dim(block, block.shape[dim] - width, None, axis=dim), axis, forward
        )
        high = lax.ppermute(lax.slice_in_dim(block, 0, width, axis=dim), axis, backward)
        block = jnp.concatenate([low, block, high], axis=dim)
    return block


def diffuse_once(extended, along_rate, cross_rate):
    center = extended[:, 1:-1]
    along_sum = extended[:, 2:] + extended[:, :-2] - 2.0 * center
    side_pad = jnp.pad(center, ((0, 0), (0, 0), (1, 1)))
    cross_sum = side_pad[:, :, 2:] + side_pad[:, :, :-2] - 2.0 * center
    return center + along_rate * along_sum + cross_rate * cross_sum


def line_rims(smooth_field):
    return extended_2(smooth_field, (("swath", 1),), 1)


def slant_of(angle_index):
    zenith = angle_index.astype(jnp.float32) * (max_zenith / (NANG - 1))
    return 1.0 / jnp.cos(zenith) - 1.0


def on_device_plain(grid_profiles, send_lists, counts, angle_index, jacobian, observed, kappa, factor):
    slot_rows = send_lists[0]
    slots = slot_rows.shape[1]
    own_chan = observed.shape[0]
    pixel_count = observed.shape[1]
    line_count = pixel_count // XTRACK
    live_slot = jnp.arange(slots, dtype=jnp.int32)[None, :] < counts[0][:, None]
    zero_value = jnp.zeros((), grid_profiles.dtype)
    outgoing = jnp.where(live_slot[:, :, None], grid_profiles[slot_rows], zero_value)
    incoming = lax.all_to_all(outgoing, "swath", split_axis=0, concat_axis=0, tiled=True)
    pixel_profiles = incoming.reshape(pixel_count, grid_profiles.shape[1])
    model = jnp.einsum("mkc,pk->mcp", jacobian, pixel_profiles, preferred_element_type=jnp.float32)
    slant_path = slant_of(angle_index)
    model = model.reshape(3, own_chan, line_count, XTRACK)
    departure = observed.astype(jnp.float32).reshape(own_chan, line_count, XTRACK) - (
        model[0] + slant_path * model[1] + slant_path * slant_path * model[2]
    )
    along_rate = kappa[0][:, None, None]
    cross_rate = kappa[1][:, None, None]
    smooth_field = departure
    for sweep in range(3):
        smooth_field = diffuse_once(line_rims(smooth_field), along_rate, cross_rate)
    smoothed = smooth_field.reshape(own_chan, pixel_count).astype(jnp.bfloat16)
    return jnp.dot(
        factor,
        lax.all_gather(smoothed, "chan", axis=0, tiled=True),
        preferred_element_type=jnp.float32,
    )


def gather_kernel(lists_ref, counts_ref, grid_ref, out_ref):
    grid_rows = grid_ref.shape[0]
    parts, slots = lists_ref.shape
    slot_number = lax.broadcasted_iota(jnp.int32, (slots, parts), 0)
    picks = jnp.where(slot_number < counts_ref[...], lists_ref[...].T, -1)
    row_number = lax.broadcasted_iota(jnp.int32, (slots, grid_rows), 1)
    for part in range(parts):
        one_hot = (picks[:, part : part + 1] == row_number).astype(jnp.float32).astype(jnp.bfloat16)
        rows = jnp.dot(one_hot, grid_ref[...], preferred_element_type=jnp.float32)
        out_ref[part] = rows.astype(out_ref.dtype)


def gather_rows(grid_profiles, slot_rows, counts):
    parts, slots = slot_rows.shape
    return pl.pallas_call(
        gather_kernel,
        out_shape=jax.ShapeDtypeStruct((parts, slots, grid_profiles.shape[1]), grid_profiles.dtype),
        compiler_params=pltpu.CompilerParams(vmem_limit_bytes=GATHER_LIMIT),
        name="pick_rows",
    )(slot_rows, counts, grid_profiles)


def half_kernel(last, *refs):
    prof_hbm, prof_top_hbm, prof_bot_hbm, top_hbm, bot_hbm, jac_hbm = refs[:6]
    if last:
        mid_hbm, bnd_hbm, smooth_hbm, factor_hbm, rates_ref, rows_ref, shift_ref = refs[6:13]
        out_hbm, prof, obs, jac_ref, field, moved_a, moved_b, smooth, sems, out_sems, out, factor_ref = refs[13:]
    else:
        obs_hbm, rates_ref, rows_ref, shift_ref = refs[6:10]
        out_hbm, prof, obs, jac_ref, field, moved_a, moved_b, smooth, sems, out_sems = refs[10:]
    own, pixels = jac_hbm.shape[1], prof_hbm.shape[0]
    rim = prof_top_hbm.shape[0]
    lines = pixels // XTRACK
    wide = 2 * XTRACK
    full = pixels + 2 * rim
    total = full // XTRACK
    first = own if last else 0
    groups = own // 16

    blocks = full // wide
    cuts = [blocks * n // SEGMENTS for n in range(SEGMENTS + 1)]
    part = pl.ds(first, own)
    waits = []
    copies = []

    def fetch(src, dst):
        copy = pltpu.make_async_copy(src, dst, sems.at[len(copies)])
        copies.append(copy)
        waits[-1].append(copy)

    for n in range(SEGMENTS):
        waits.append([])
        if n == 0:
            fetch(jac_hbm, jac_ref)
            fetch(prof_top_hbm, prof.at[pl.ds(0, rim), :])
            fetch(top_hbm.at[part, :], obs.at[:, pl.ds(0, rim)])
        low = max(cuts[n] * wide - rim, 0)
        high = min(cuts[n + 1] * wide - rim, pixels)
        fetch(prof_hbm.at[pl.ds(low, high - low), :], prof.at[pl.ds(rim + low, high - low), :])
        if last:
            spans = [(bnd_hbm, 0, 0, rim), (mid_hbm, 0, rim, pixels - rim), (bnd_hbm, rim, pixels - rim, pixels)]
        else:
            spans = [(obs_hbm, 0, 0, pixels)]
        for src, origin, begin, end in spans:
            begin_n, end_n = max(begin, low), min(end, high)
            if begin_n < end_n:
                fetch(
                    src.at[:, pl.ds(origin + begin_n - begin, end_n - begin_n)],
                    obs.at[:, pl.ds(rim + begin_n, end_n - begin_n)],
                )
        if n == SEGMENTS - 1:
            fetch(prof_bot_hbm, prof.at[pl.ds(rim + pixels, rim), :])
            fetch(bot_hbm.at[part, :], obs.at[:, pl.ds(rim + pixels, rim)])
    if last:
        waits.append([])
        fetch(smooth_hbm, smooth.at[pl.ds(0, own), :])
        fetch(factor_hbm, factor_ref)

    def start(n):
        for copy in waits[n] if n < len(waits) else []:
            copy.start()

    for n in range(AHEAD):
        start(n)
    s1 = jnp.concatenate([rows_ref[0:1, :]] * 2, axis=1)
    s2 = jnp.concatenate([rows_ref[1:2, :]] * 2, axis=1)
    inside_top = rows_ref[2:3, :]
    inside_bot = rows_ref[3:4, :]

    def departures(t):
        at = pl.multiple_of(t * wide, wide)
        here = prof[pl.ds(at, wide), :]
        terms = [
            lax.dot_general(jac_ref[m], here, (((1,), (1,)), ((), ())), preferred_element_type=jnp.float32)
            for m in range(3)
        ]
        field[:, pl.ds(at, wide)] = obs[:, pl.ds(at, wide)].astype(jnp.float32) - (
            terms[0] + s1 * terms[1] + s2 * terms[2]
        )

    def shifts(i, moved):
        rows = pl.ds(pl.multiple_of(i * 16, 16), 16)
        tiles = []
        for j in range(1, total - 1):
            here = field[rows, j * XTRACK : (j + 1) * XTRACK]
            high = here.astype(jnp.bfloat16)
            low = (here - high.astype(jnp.float32)).astype(jnp.bfloat16)
            tiles.append(jnp.concatenate([high, low], axis=1))
        moved[...] = jnp.dot(
            jnp.concatenate(tiles, axis=0), shift_ref[...], preferred_element_type=jnp.float32
        )

    def sweeps(i, moved):
        rows = pl.ds(pl.multiple_of(i * 16, 16), 16)
        chan = pl.ds(pl.multiple_of(first + i * 16, 16), 16)
        along = jnp.broadcast_to(rates_ref[rows, 0:1], (16, XTRACK))
        cross = jnp.broadcast_to(rates_ref[rows, 1:2], (16, XTRACK))
        stay = 1.0 - 2.0 * along - 2.0 * cross
        cross = [3.0 * cross, 3.0 * cross * cross, cross * cross * cross]
        fields = [{}, {}, {}, {}]
        for j in range(total):
            fields[0][j] = field[rows, j * XTRACK : (j + 1) * XTRACK]
            for k in range(1, HALO + 1):
                at = j - k
                if at < k:
                    continue
                prev = fields[k - 1]
                new = (
                    stay * prev[at]
                    + along * (prev[at - 1] + prev[at + 1])
                    + cross[k - 1] * moved[(at - 1) * 16 : at * 16, (k - 1) * XTRACK : k * XTRACK]
                )
                if at < HALO:
                    new = new * inside_top
                if at >= HALO + lines:
                    new = new * inside_bot
                fields[k][at] = new
                del prev[at - 1]
                if k == HALO:
                    line = at - HALO
                    smooth[chan, line * XTRACK : (line + 1) * XTRACK] = new.astype(smooth.dtype)

    for n in range(SEGMENTS):
        for copy in waits[n]:
            copy.wait()
        start(n + AHEAD)
        pl.loop(cuts[n], cuts[n + 1], unroll=cuts[n + 1] - cuts[n])(departures)

    def smooth_copy(n, size):
        rows = pl.ds(pl.multiple_of(n, 16), size)
        return pltpu.make_async_copy(smooth.at[rows, :], out_hbm.at[rows, :], out_sems.at[0])

    shifts(0, moved_a)

    @pl.loop(0, groups // 2, unroll=groups // 2)
    def _(h):
        shifts(2 * h + 1, moved_b)
        sweeps(2 * h, moved_a)
        shifts(jnp.minimum(2 * h + 2, groups - 1), moved_a)
        sweeps(2 * h + 1, moved_b)
        if not last:
            smooth_copy(32 * h, 32).start()

    if groups % 2:
        sweeps(groups - 1, moved_a)
        if not last:
            smooth_copy(16 * (groups - 1), 16).start()

    if not last:
        smooth_copy(0, own).wait()
        return

    for copy in waits[SEGMENTS]:
        copy.wait()

    def out_copy(t):
        at = pl.multiple_of(t * OUT_BLOCK, OUT_BLOCK)
        return pltpu.make_async_copy(
            out.at[:, pl.ds(at, OUT_BLOCK)], out_hbm.at[:, pl.ds(at, OUT_BLOCK)], out_sems.at[t]
        )

    @pl.loop(0, pixels // OUT_BLOCK, unroll=pixels // OUT_BLOCK)
    def _(t):
        at = pl.multiple_of(t * OUT_BLOCK, OUT_BLOCK)
        out[:, pl.ds(at, OUT_BLOCK)] = jnp.dot(
            factor_ref[...], smooth[:, pl.ds(at, OUT_BLOCK)], preferred_element_type=jnp.float32
        )
        out_copy(t).start()

    pl.loop(0, pixels // OUT_BLOCK)(lambda t: out_copy(t).wait())


def half_call(last, anys, whole):
    own, pixels = anys[5].shape[1], anys[0].shape[0]
    rim = anys[1].shape[0]
    full = pixels + 2 * rim
    dtype = jnp.float32 if last else jnp.bfloat16
    scratch = [
        pltpu.VMEM((full, anys[0].shape[1]), jnp.bfloat16),
        pltpu.VMEM((own, full), jnp.bfloat16),
        pltpu.VMEM(anys[5].shape, jnp.bfloat16),
        pltpu.VMEM((own, full), jnp.float32),
        pltpu.VMEM((16 * (full // XTRACK - 2), HALO * XTRACK), jnp.float32),
        pltpu.VMEM((16 * (full // XTRACK - 2), HALO * XTRACK), jnp.float32),
        pltpu.VMEM((2 * own if last else own, pixels), jnp.bfloat16),
        pltpu.SemaphoreType.DMA((32,)),
        pltpu.SemaphoreType.DMA((pixels // OUT_BLOCK,)),
    ]
    if last:
        scratch += [pltpu.VMEM((own, pixels), jnp.float32), pltpu.VMEM((own, 2 * own), jnp.bfloat16)]
    return pl.pallas_call(
        functools.partial(half_kernel, last),
        out_shape=jax.ShapeDtypeStruct((own, pixels), dtype),
        in_specs=[pl.BlockSpec(memory_space=pl.ANY)] * len(anys)
        + [pl.BlockSpec(memory_space=pltpu.VMEM)] * len(whole),
        out_specs=pl.BlockSpec(memory_space=pl.ANY),
        scratch_shapes=scratch,
        compiler_params=pltpu.CompilerParams(vmem_limit_bytes=LAST_LIMIT if last else OWN_LIMIT),
        name="other_half_and_factor" if last else "own_half",
    )(*anys, *whole)


def on_device_two(grid_profiles, send_lists, counts, angle_index, jacobian, observed, kappa, factor):
    own, pixels = observed.shape
    rim = HALO * XTRACK
    swath = lax.axis_size("swath")
    place = lax.axis_index("swath")
    half = lax.axis_index("chan")
    swap = [(0, 1), (1, 0)]
    forward = [(i, i + 1) for i in range(swath - 1)]
    backward = [(i + 1, i) for i in range(swath - 1)]

    def halos(block, axis):
        size = block.shape[axis]
        tail = lax.slice_in_dim(block, size - rim, size, axis=axis)
        head = lax.slice_in_dim(block, 0, rim, axis=axis)
        return lax.ppermute(tail, "swath", forward), lax.ppermute(head, "swath", backward)

    jac_own = jnp.swapaxes(jacobian, 1, 2)
    jac_half = lax.dynamic_slice_in_dim(jac_own, (place % 2) * (own // 2), own // 2, axis=1)
    jac_near = lax.ppermute(jac_half, "chan", swap)
    rates_own = kappa.T
    rates_oth = lax.ppermute(rates_own, "chan", swap)
    outgoing = gather_rows(grid_profiles, send_lists[0], counts)
    outgoing, obs_late = lax.optimization_barrier((outgoing, observed))
    bnd_own = jnp.concatenate([obs_late[:, :rim], obs_late[:, pixels - rim :]], axis=1)
    bnd_oth = lax.ppermute(bnd_own, "chan", swap)
    incoming = lax.all_to_all(outgoing, "swath", split_axis=0, concat_axis=0, tiled=True)
    middle = obs_late[:, rim : pixels - rim]
    middle, jac_near, bnd_oth = lax.optimization_barrier((middle, jac_near, bnd_oth))
    mid_oth = lax.ppermute(middle, "chan", swap)
    jac_far = lax.ppermute(jac_near, "swath", [(i, i ^ 1) for i in range(swath)])
    jac_oth = jnp.where(
        place % 2 == 0,
        jnp.concatenate([jac_near, jac_far], axis=1),
        jnp.concatenate([jac_far, jac_near], axis=1),
    )
    near = np.eye(XTRACK, k=1) + np.eye(XTRACK, k=-1)
    moves = np.concatenate([near, near @ near, near @ near @ near], axis=1)
    shift = jnp.asarray(np.concatenate([moves, moves], axis=0), jnp.bfloat16)
    slant = slant_of(angle_index)
    ones = jnp.ones((XTRACK,), jnp.float32)
    rows = jnp.stack([
        slant,
        slant * slant,
        jnp.where(place > 0, ones, 0.0),
        jnp.where(place < swath - 1, ones, 0.0),
    ])
    factor_two = jnp.where(half == 0, factor, jnp.roll(factor, own, axis=1))

    bnd_own, bnd_oth, jac_oth, rates_oth, rows, factor_two = lax.optimization_barrier(
        (bnd_own, bnd_oth, jac_oth, rates_oth, rows, factor_two)
    )
    bnd_both = jnp.concatenate([bnd_own, bnd_oth], axis=0)
    obs_top = lax.ppermute(bnd_both[:, rim:], "swath", forward)
    obs_bot = lax.ppermute(bnd_both[:, :rim], "swath", backward)

    profiles = incoming.reshape(pixels, grid_profiles.shape[1])
    prof_halos = halos(profiles, 0)

    smooth_own = half_call(
        False,
        (profiles, *prof_halos, obs_top, obs_bot, jac_own, observed),
        (rates_own, rows, shift),
    )
    return half_call(
        True,
        (profiles, *prof_halos, obs_top, obs_bot, jac_oth, mid_oth, bnd_oth, smooth_own, factor_two),
        (rates_oth, rows, shift),
    )


def solution(mesh):
    in_specs = (
        P("swath", None),
        P("swath", None, None),
        P("swath", None),
        P(),
        P(None, None, "chan"),
        P("chan", "swath"),
        P(None, "chan"),
        P("chan", None),
    )
    out_specs = P("chan", "swath")
    on_device = on_device_two if mesh.shape["chan"] == 2 else on_device_plain
    return jax.shard_map(
        on_device, mesh=mesh, in_specs=in_specs, out_specs=out_specs, check_vma=False
    )
```

```python
import functools
import math

import jax
import jax.numpy as jnp
import numpy as np
from jax import lax
from jax.experimental import pallas as pl
from jax.experimental.pallas import tpu as pltpu
from jax.sharding import PartitionSpec as P

XTRACK = 128
NANG = 8
HALO = 3
OUT_BLOCK = 512
GATHER_LIMIT = 60 * 1024 * 1024
OWN_LIMIT = 60 * 1024 * 1024
LAST_LIMIT = 60 * 1024 * 1024
SEGMENTS = 4
AHEAD = 2


max_zenith = math.pi / 3.0


def extended_2(block, sides, width):
    for axis, dim in sides:
        count = lax.axis_size(axis)
        forward = [(i, i + 1) for i in range(count - 1)]
        backward = [(target, source) for source, target in forward]
        low = lax.ppermute(
            lax.slice_in_dim(block, block.shape[dim] - width, None, axis=dim), axis, forward
        )
        high = lax.ppermute(lax.slice_in_dim(block, 0, width, axis=dim), axis, backward)
        block = jnp.concatenate([low, block, high], axis=dim)
    return block


def diffuse_once(extended, along_rate, cross_rate):
    center = extended[:, 1:-1]
    along_sum = extended[:, 2:] + extended[:, :-2] - 2.0 * center
    side_pad = jnp.pad(center, ((0, 0), (0, 0), (1, 1)))
    cross_sum = side_pad[:, :, 2:] + side_pad[:, :, :-2] - 2.0 * center
    return center + along_rate * along_sum + cross_rate * cross_sum


def line_rims(smooth_field):
    return extended_2(smooth_field, (("swath", 1),), 1)


def slant_of(angle_index):
    zenith = angle_index.astype(jnp.float32) * (max_zenith / (NANG - 1))
    return 1.0 / jnp.cos(zenith) - 1.0


def on_device_plain(grid_profiles, send_lists, counts, angle_index, jacobian, observed, kappa, factor):
    slot_rows = send_lists[0]
    slots = slot_rows.shape[1]
    own_chan = observed.shape[0]
    pixel_count = observed.shape[1]
    line_count = pixel_count // XTRACK
    live_slot = jnp.arange(slots, dtype=jnp.int32)[None, :] < counts[0][:, None]
    zero_value = jnp.zeros((), grid_profiles.dtype)
    outgoing = jnp.where(live_slot[:, :, None], grid_profiles[slot_rows], zero_value)
    incoming = lax.all_to_all(outgoing, "swath", split_axis=0, concat_axis=0, tiled=True)
    pixel_profiles = incoming.reshape(pixel_count, grid_profiles.shape[1])
    model = jnp.einsum("mkc,pk->mcp", jacobian, pixel_profiles, preferred_element_type=jnp.float32)
    slant_path = slant_of(angle_index)
    model = model.reshape(3, own_chan, line_count, XTRACK)
    departure = observed.astype(jnp.float32).reshape(own_chan, line_count, XTRACK) - (
        model[0] + slant_path * model[1] + slant_path * slant_path * model[2]
    )
    along_rate = kappa[0][:, None, None]
    cross_rate = kappa[1][:, None, None]
    smooth_field = departure
    for sweep in range(3):
        smooth_field = diffuse_once(line_rims(smooth_field), along_rate, cross_rate)
    smoothed = smooth_field.reshape(own_chan, pixel_count).astype(jnp.bfloat16)
    return jnp.dot(
        factor,
        lax.all_gather(smoothed, "chan", axis=0, tiled=True),
        preferred_element_type=jnp.float32,
    )


def gather_kernel(lists_hbm, counts_hbm, grid_hbm, out_hbm, lists, counts, grid, out, sems, out_sem):
    ins = [(lists_hbm, lists), (counts_hbm, counts), (grid_hbm, grid)]
    ins = [pltpu.make_async_copy(src, dst, sems.at[n]) for n, (src, dst) in enumerate(ins)]
    for copy in ins:
        copy.start()
    for copy in ins[:2]:
        copy.wait()
    grid_rows = grid.shape[0]
    parts, slots = lists.shape
    slot_number = lax.broadcasted_iota(jnp.int32, (slots, parts), 0)
    picks = jnp.where(slot_number < counts[...], lists[...].T, -1)
    row_number = lax.broadcasted_iota(jnp.int32, (slots, grid_rows), 1)
    ins[2].wait()
    for part in range(parts):
        one_hot = (picks[:, part : part + 1] == row_number).astype(jnp.float32).astype(jnp.bfloat16)
        rows = jnp.dot(one_hot, grid[...], preferred_element_type=jnp.float32)
        out[part] = rows.astype(out.dtype)
        pltpu.make_async_copy(out.at[part], out_hbm.at[part], out_sem).start()
    pltpu.make_async_copy(out, out_hbm, out_sem).wait()


def gather_rows(grid_profiles, slot_rows, counts):
    parts, slots = slot_rows.shape
    shape = (parts, slots, grid_profiles.shape[1])
    return pl.pallas_call(
        gather_kernel,
        out_shape=jax.ShapeDtypeStruct(shape, grid_profiles.dtype),
        in_specs=[pl.BlockSpec(memory_space=pl.ANY)] * 3,
        out_specs=pl.BlockSpec(memory_space=pl.ANY),
        scratch_shapes=[
            pltpu.VMEM(slot_rows.shape, jnp.int32),
            pltpu.VMEM(counts.shape, jnp.int32),
            pltpu.VMEM(grid_profiles.shape, grid_profiles.dtype),
            pltpu.VMEM(shape, grid_profiles.dtype),
            pltpu.SemaphoreType.DMA((3,)),
            pltpu.SemaphoreType.DMA,
        ],
        compiler_params=pltpu.CompilerParams(vmem_limit_bytes=GATHER_LIMIT),
        name="pick_rows",
    )(slot_rows, counts, grid_profiles)


def half_kernel(last, *refs):
    prof_hbm, prof_top_hbm, prof_bot_hbm, top_hbm, bot_hbm, jac_hbm = refs[:6]
    if last:
        mid_hbm, bnd_hbm, smooth_hbm, factor_hbm, rates_ref, rows_ref, shift_ref = refs[6:13]
        out_hbm, prof, obs, jac_ref, field, moved_a, moved_b, smooth, sems, out_sems, out, factor_ref = refs[13:]
    else:
        obs_hbm, rates_ref, rows_ref, shift_ref = refs[6:10]
        out_hbm, prof, obs, jac_ref, field, moved_a, moved_b, smooth, sems, out_sems = refs[10:]
    own, pixels = jac_hbm.shape[1], prof_hbm.shape[0]
    rim = prof_top_hbm.shape[0]
    lines = pixels // XTRACK
    wide = 2 * XTRACK
    full = pixels + 2 * rim
    total = full // XTRACK
    first = own if last else 0
    groups = own // 16

    blocks = full // wide
    cuts = [blocks * n // SEGMENTS for n in range(SEGMENTS + 1)]
    part = pl.ds(first, own)
    waits = []
    copies = []

    def fetch(src, dst):
        copy = pltpu.make_async_copy(src, dst, sems.at[len(copies)])
        copies.append(copy)
        waits[-1].append(copy)

    for n in range(SEGMENTS):
        waits.append([])
        if n == 0:
            fetch(jac_hbm, jac_ref)
            fetch(prof_top_hbm, prof.at[pl.ds(0, rim), :])
            fetch(top_hbm.at[part, :], obs.at[:, pl.ds(0, rim)])
        low = max(cuts[n] * wide - rim, 0)
        high = min(cuts[n + 1] * wide - rim, pixels)
        fetch(prof_hbm.at[pl.ds(low, high - low), :], prof.at[pl.ds(rim + low, high - low), :])
        if last:
            spans = [(bnd_hbm, 0, 0, rim), (mid_hbm, 0, rim, pixels - rim), (bnd_hbm, rim, pixels - rim, pixels)]
        else:
            spans = [(obs_hbm, 0, 0, pixels)]
        for src, origin, begin, end in spans:
            begin_n, end_n = max(begin, low), min(end, high)
            if begin_n < end_n:
                fetch(
                    src.at[:, pl.ds(origin + begin_n - begin, end_n - begin_n)],
                    obs.at[:, pl.ds(rim + begin_n, end_n - begin_n)],
                )
        if n == SEGMENTS - 1:
            fetch(prof_bot_hbm, prof.at[pl.ds(rim + pixels, rim), :])
            fetch(bot_hbm.at[part, :], obs.at[:, pl.ds(rim + pixels, rim)])
    if last:
        waits.append([])
        fetch(smooth_hbm, smooth.at[pl.ds(0, own), :])
        fetch(factor_hbm, factor_ref)

    def start(n):
        for copy in waits[n] if n < len(waits) else []:
            copy.start()

    for n in range(AHEAD):
        start(n)
    s1 = jnp.concatenate([rows_ref[0:1, :]] * 2, axis=1)
    s2 = jnp.concatenate([rows_ref[1:2, :]] * 2, axis=1)
    inside_top = rows_ref[2:3, :]
    inside_bot = rows_ref[3:4, :]

    def departures(t):
        at = pl.multiple_of(t * wide, wide)
        here = prof[pl.ds(at, wide), :]
        terms = [
            lax.dot_general(jac_ref[m], here, (((1,), (1,)), ((), ())), preferred_element_type=jnp.float32)
            for m in range(3)
        ]
        field[:, pl.ds(at, wide)] = obs[:, pl.ds(at, wide)].astype(jnp.float32) - (
            terms[0] + s1 * terms[1] + s2 * terms[2]
        )

    def shifts(i, moved):
        rows = pl.ds(pl.multiple_of(i * 16, 16), 16)
        tiles = []
        for j in range(1, total - 1):
            here = field[rows, j * XTRACK : (j + 1) * XTRACK]
            high = here.astype(jnp.bfloat16)
            low = (here - high.astype(jnp.float32)).astype(jnp.bfloat16)
            tiles.append(jnp.concatenate([high, low], axis=1))
        moved[...] = jnp.dot(
            jnp.concatenate(tiles, axis=0), shift_ref[...], preferred_element_type=jnp.float32
        )

    def sweeps(i, moved):
        rows = pl.ds(pl.multiple_of(i * 16, 16), 16)
        chan = pl.ds(pl.multiple_of(first + i * 16, 16), 16)
        along = jnp.broadcast_to(rates_ref[rows, 0:1], (16, XTRACK))
        cross = jnp.broadcast_to(rates_ref[rows, 1:2], (16, XTRACK))
        stay = 1.0 - 2.0 * along - 2.0 * cross
        cross = [3.0 * cross, 3.0 * cross * cross, cross * cross * cross]
        fields = [{}, {}, {}, {}]
        for j in range(total):
            fields[0][j] = field[rows, j * XTRACK : (j + 1) * XTRACK]
            for k in range(1, HALO + 1):
                at = j - k
                if at < k:
                    continue
                prev = fields[k - 1]
                new = (
                    stay * prev[at]
                    + along * (prev[at - 1] + prev[at + 1])
                    + cross[k - 1] * moved[(at - 1) * 16 : at * 16, (k - 1) * XTRACK : k * XTRACK]
                )
                if at < HALO:
                    new = new * inside_top
                if at >= HALO + lines:
                    new = new * inside_bot
                fields[k][at] = new
                del prev[at - 1]
                if k == HALO:
                    line = at - HALO
                    smooth[chan, line * XTRACK : (line + 1) * XTRACK] = new.astype(smooth.dtype)

    for n in range(SEGMENTS):
        for copy in waits[n]:
            copy.wait()
        start(n + AHEAD)
        pl.loop(cuts[n], cuts[n + 1], unroll=cuts[n + 1] - cuts[n])(departures)

    def smooth_copy(n, size):
        rows = pl.ds(pl.multiple_of(n, 16), size)
        return pltpu.make_async_copy(smooth.at[rows, :], out_hbm.at[rows, :], out_sems.at[0])

    shifts(0, moved_a)

    @pl.loop(0, groups // 2, unroll=groups // 2)
    def _(h):
        shifts(2 * h + 1, moved_b)
        sweeps(2 * h, moved_a)
        shifts(jnp.minimum(2 * h + 2, groups - 1), moved_a)
        sweeps(2 * h + 1, moved_b)
        if not last:
            smooth_copy(32 * h, 32).start()

    if groups % 2:
        sweeps(groups - 1, moved_a)
        if not last:
            smooth_copy(16 * (groups - 1), 16).start()

    if not last:
        smooth_copy(0, own).wait()
        return

    for copy in waits[SEGMENTS]:
        copy.wait()

    def out_copy(t):
        at = pl.multiple_of(t * OUT_BLOCK, OUT_BLOCK)
        return pltpu.make_async_copy(
            out.at[:, pl.ds(at, OUT_BLOCK)], out_hbm.at[:, pl.ds(at, OUT_BLOCK)], out_sems.at[t]
        )

    @pl.loop(0, pixels // OUT_BLOCK, unroll=pixels // OUT_BLOCK)
    def _(t):
        at = pl.multiple_of(t * OUT_BLOCK, OUT_BLOCK)
        out[:, pl.ds(at, OUT_BLOCK)] = jnp.dot(
            factor_ref[...], smooth[:, pl.ds(at, OUT_BLOCK)], preferred_element_type=jnp.float32
        )
        out_copy(t).start()

    pl.loop(0, pixels // OUT_BLOCK)(lambda t: out_copy(t).wait())


def half_call(last, anys, whole):
    own, pixels = anys[5].shape[1], anys[0].shape[0]
    rim = anys[1].shape[0]
    full = pixels + 2 * rim
    dtype = jnp.float32 if last else jnp.bfloat16
    scratch = [
        pltpu.VMEM((full, anys[0].shape[1]), jnp.bfloat16),
        pltpu.VMEM((own, full), jnp.bfloat16),
        pltpu.VMEM(anys[5].shape, jnp.bfloat16),
        pltpu.VMEM((own, full), jnp.float32),
        pltpu.VMEM((16 * (full // XTRACK - 2), HALO * XTRACK), jnp.float32),
        pltpu.VMEM((16 * (full // XTRACK - 2), HALO * XTRACK), jnp.float32),
        pltpu.VMEM((2 * own if last else own, pixels), jnp.bfloat16),
        pltpu.SemaphoreType.DMA((32,)),
        pltpu.SemaphoreType.DMA((pixels // OUT_BLOCK,)),
    ]
    if last:
        scratch += [pltpu.VMEM((own, pixels), jnp.float32), pltpu.VMEM((own, 2 * own), jnp.bfloat16)]
    return pl.pallas_call(
        functools.partial(half_kernel, last),
        out_shape=jax.ShapeDtypeStruct((own, pixels), dtype),
        in_specs=[pl.BlockSpec(memory_space=pl.ANY)] * len(anys)
        + [pl.BlockSpec(memory_space=pltpu.VMEM)] * len(whole),
        out_specs=pl.BlockSpec(memory_space=pl.ANY),
        scratch_shapes=scratch,
        compiler_params=pltpu.CompilerParams(vmem_limit_bytes=LAST_LIMIT if last else OWN_LIMIT),
        name="other_half_and_factor" if last else "own_half",
    )(*anys, *whole)


def on_device_two(grid_profiles, send_lists, counts, angle_index, jacobian, observed, kappa, factor):
    own, pixels = observed.shape
    rim = HALO * XTRACK
    swath = lax.axis_size("swath")
    place = lax.axis_index("swath")
    half = lax.axis_index("chan")
    swap = [(0, 1), (1, 0)]
    forward = [(i, i + 1) for i in range(swath - 1)]
    backward = [(i + 1, i) for i in range(swath - 1)]

    def halos(block, axis):
        size = block.shape[axis]
        tail = lax.slice_in_dim(block, size - rim, size, axis=axis)
        head = lax.slice_in_dim(block, 0, rim, axis=axis)
        return lax.ppermute(tail, "swath", forward), lax.ppermute(head, "swath", backward)

    jac_own = jnp.swapaxes(jacobian, 1, 2)
    jac_half = lax.dynamic_slice_in_dim(jac_own, (place % 2) * (own // 2), own // 2, axis=1)
    jac_near = lax.ppermute(jac_half, "chan", swap)
    rates_own = kappa.T
    rates_oth = lax.ppermute(rates_own, "chan", swap)
    outgoing = gather_rows(grid_profiles, send_lists[0], counts)
    outgoing, obs_late = lax.optimization_barrier((outgoing, observed))
    bnd_own = jnp.concatenate([obs_late[:, :rim], obs_late[:, pixels - rim :]], axis=1)
    bnd_oth = lax.ppermute(bnd_own, "chan", swap)
    incoming = lax.all_to_all(outgoing, "swath", split_axis=0, concat_axis=0, tiled=True)
    middle = obs_late[:, rim : pixels - rim]
    middle, bnd_oth = lax.optimization_barrier((middle, bnd_oth))
    mid_oth = lax.ppermute(middle, "chan", swap)
    jac_far = lax.ppermute(jac_near, "swath", [(i, i ^ 1) for i in range(swath)])
    jac_oth = jnp.where(
        place % 2 == 0,
        jnp.concatenate([jac_near, jac_far], axis=1),
        jnp.concatenate([jac_far, jac_near], axis=1),
    )
    near = np.eye(XTRACK, k=1) + np.eye(XTRACK, k=-1)
    moves = np.concatenate([near, near @ near, near @ near @ near], axis=1)
    shift = jnp.asarray(np.concatenate([moves, moves], axis=0), jnp.bfloat16)
    slant = slant_of(angle_index)
    ones = jnp.ones((XTRACK,), jnp.float32)
    rows = jnp.stack([
        slant,
        slant * slant,
        jnp.where(place > 0, ones, 0.0),
        jnp.where(place < swath - 1, ones, 0.0),
    ])
    factor_two = jnp.where(half == 0, factor, jnp.roll(factor, own, axis=1))

    bnd_own, bnd_oth, jac_oth, rates_oth, rows, factor_two = lax.optimization_barrier(
        (bnd_own, bnd_oth, jac_oth, rates_oth, rows, factor_two)
    )
    bnd_both = jnp.concatenate([bnd_own, bnd_oth], axis=0)
    obs_top = lax.ppermute(bnd_both[:, rim:], "swath", forward)
    obs_bot = lax.ppermute(bnd_both[:, :rim], "swath", backward)

    profiles = incoming.reshape(pixels, grid_profiles.shape[1])
    prof_halos = halos(profiles, 0)

    smooth_own = half_call(
        False,
        (profiles, *prof_halos, obs_top, obs_bot, jac_own, observed),
        (rates_own, rows, shift),
    )
    return half_call(
        True,
        (profiles, *prof_halos, obs_top, obs_bot, jac_oth, mid_oth, bnd_oth, smooth_own, factor_two),
        (rates_oth, rows, shift),
    )


def solution(mesh):
    in_specs = (
        P("swath", None),
        P("swath", None, None),
        P("swath", None),
        P(),
        P(None, None, "chan"),
        P("chan", "swath"),
        P(None, "chan"),
        P("chan", None),
    )
    out_specs = P("chan", "swath")
    on_device = on_device_two if mesh.shape["chan"] == 2 else on_device_plain
    return jax.shard_map(
        on_device, mesh=mesh, in_specs=in_specs, out_specs=out_specs, check_vma=False
    )
```

```python
import functools
import math

import jax
import jax.numpy as jnp
import numpy as np
from jax import lax
from jax.experimental import pallas as pl
from jax.experimental.pallas import tpu as pltpu
from jax.sharding import PartitionSpec as P

XTRACK = 128
NANG = 8
HALO = 3
OUT_BLOCK = 512
GATHER_LIMIT = 60 * 1024 * 1024
OWN_LIMIT = 60 * 1024 * 1024
LAST_LIMIT = 60 * 1024 * 1024
SEGMENTS = 4
AHEAD = 2


max_zenith = math.pi / 3.0


def extended_2(block, sides, width):
    for axis, dim in sides:
        count = lax.axis_size(axis)
        forward = [(i, i + 1) for i in range(count - 1)]
        backward = [(target, source) for source, target in forward]
        low = lax.ppermute(
            lax.slice_in_dim(block, block.shape[dim] - width, None, axis=dim), axis, forward
        )
        high = lax.ppermute(lax.slice_in_dim(block, 0, width, axis=dim), axis, backward)
        block = jnp.concatenate([low, block, high], axis=dim)
    return block


def diffuse_once(extended, along_rate, cross_rate):
    center = extended[:, 1:-1]
    along_sum = extended[:, 2:] + extended[:, :-2] - 2.0 * center
    side_pad = jnp.pad(center, ((0, 0), (0, 0), (1, 1)))
    cross_sum = side_pad[:, :, 2:] + side_pad[:, :, :-2] - 2.0 * center
    return center + along_rate * along_sum + cross_rate * cross_sum


def line_rims(smooth_field):
    return extended_2(smooth_field, (("swath", 1),), 1)


def slant_of(angle_index):
    zenith = angle_index.astype(jnp.float32) * (max_zenith / (NANG - 1))
    return 1.0 / jnp.cos(zenith) - 1.0


def on_device_plain(grid_profiles, send_lists, counts, angle_index, jacobian, observed, kappa, factor):
    slot_rows = send_lists[0]
    slots = slot_rows.shape[1]
    own_chan = observed.shape[0]
    pixel_count = observed.shape[1]
    line_count = pixel_count // XTRACK
    live_slot = jnp.arange(slots, dtype=jnp.int32)[None, :] < counts[0][:, None]
    zero_value = jnp.zeros((), grid_profiles.dtype)
    outgoing = jnp.where(live_slot[:, :, None], grid_profiles[slot_rows], zero_value)
    incoming = lax.all_to_all(outgoing, "swath", split_axis=0, concat_axis=0, tiled=True)
    pixel_profiles = incoming.reshape(pixel_count, grid_profiles.shape[1])
    model = jnp.einsum("mkc,pk->mcp", jacobian, pixel_profiles, preferred_element_type=jnp.float32)
    slant_path = slant_of(angle_index)
    model = model.reshape(3, own_chan, line_count, XTRACK)
    departure = observed.astype(jnp.float32).reshape(own_chan, line_count, XTRACK) - (
        model[0] + slant_path * model[1] + slant_path * slant_path * model[2]
    )
    along_rate = kappa[0][:, None, None]
    cross_rate = kappa[1][:, None, None]
    smooth_field = departure
    for sweep in range(3):
        smooth_field = diffuse_once(line_rims(smooth_field), along_rate, cross_rate)
    smoothed = smooth_field.reshape(own_chan, pixel_count).astype(jnp.bfloat16)
    return jnp.dot(
        factor,
        lax.all_gather(smoothed, "chan", axis=0, tiled=True),
        preferred_element_type=jnp.float32,
    )


def gather_kernel(lists_hbm, counts_hbm, grid_hbm, out_hbm, lists, counts, grid, out, sems, out_sem):
    ins = [(lists_hbm, lists), (counts_hbm, counts), (grid_hbm, grid)]
    ins = [pltpu.make_async_copy(src, dst, sems.at[n]) for n, (src, dst) in enumerate(ins)]
    for copy in ins:
        copy.start()
    for copy in ins[:2]:
        copy.wait()
    grid_rows = grid.shape[0]
    parts, slots = lists.shape
    slot_number = lax.broadcasted_iota(jnp.int32, (slots, parts), 0)
    picks = jnp.where(slot_number < counts[...], lists[...].T, -1)
    row_number = lax.broadcasted_iota(jnp.int32, (slots, grid_rows), 1)
    ins[2].wait()
    for part in range(parts):
        one_hot = (picks[:, part : part + 1] == row_number).astype(jnp.float32).astype(jnp.bfloat16)
        rows = jnp.dot(one_hot, grid[...], preferred_element_type=jnp.float32)
        out[part] = rows.astype(out.dtype)
        pltpu.make_async_copy(out.at[part], out_hbm.at[part], out_sem).start()
    pltpu.make_async_copy(out, out_hbm, out_sem).wait()


def gather_rows(grid_profiles, slot_rows, counts):
    parts, slots = slot_rows.shape
    shape = (parts, slots, grid_profiles.shape[1])
    return pl.pallas_call(
        gather_kernel,
        out_shape=jax.ShapeDtypeStruct(shape, grid_profiles.dtype),
        in_specs=[pl.BlockSpec(memory_space=pl.ANY)] * 3,
        out_specs=pl.BlockSpec(memory_space=pl.ANY),
        scratch_shapes=[
            pltpu.VMEM(slot_rows.shape, jnp.int32),
            pltpu.VMEM(counts.shape, jnp.int32),
            pltpu.VMEM(grid_profiles.shape, grid_profiles.dtype),
            pltpu.VMEM(shape, grid_profiles.dtype),
            pltpu.SemaphoreType.DMA((3,)),
            pltpu.SemaphoreType.DMA,
        ],
        compiler_params=pltpu.CompilerParams(vmem_limit_bytes=GATHER_LIMIT),
        name="pick_rows",
    )(slot_rows, counts, grid_profiles)


def half_kernel(last, *refs):
    prof_hbm, prof_near_hbm, prof_next_hbm, top_hbm, bot_hbm, jac_hbm = refs[:6]
    if last:
        mid_hbm, bnd_hbm, smooth_hbm, factor_hbm, odd_ref, rates_ref, rows_ref, shift_ref = refs[6:14]
        out_hbm, prof, obs, jac_ref, field, moved_a, moved_b, smooth, sems, out_sems, out, factor_ref = refs[14:]
    else:
        obs_hbm, odd_ref, rates_ref, rows_ref, shift_ref = refs[6:11]
        out_hbm, prof, obs, jac_ref, field, moved_a, moved_b, smooth, sems, out_sems = refs[11:]
    own, pixels = jac_hbm.shape[1], prof_hbm.shape[0]
    rim = prof_near_hbm.shape[0]
    lines = pixels // XTRACK
    wide = 2 * XTRACK
    full = pixels + 2 * rim
    total = full // XTRACK
    first = own if last else 0
    groups = own // 16

    blocks = full // wide
    cuts = [blocks * n // SEGMENTS for n in range(SEGMENTS + 1)]
    part = pl.ds(first, own)
    waits = []
    copies = []

    def fetch(src, dst):
        copy = pltpu.make_async_copy(src, dst, sems.at[len(copies)])
        copies.append(copy)
        waits[-1].append(copy)

    for n in range(SEGMENTS):
        waits.append([])
        if n == 0:
            fetch(jac_hbm, jac_ref)
            for src, number in ((prof_near_hbm, 1 - odd_ref[0]), (prof_next_hbm, odd_ref[0])):
                fetch(src, prof.at[pl.ds(pl.multiple_of(number * (rim + pixels), XTRACK), rim), :])
            fetch(top_hbm.at[part, :], obs.at[:, pl.ds(0, rim)])
        low = max(cuts[n] * wide - rim, 0)
        high = min(cuts[n + 1] * wide - rim, pixels)
        fetch(prof_hbm.at[pl.ds(low, high - low), :], prof.at[pl.ds(rim + low, high - low), :])
        if last:
            spans = [(bnd_hbm, 0, 0, rim), (mid_hbm, 0, rim, pixels - rim), (bnd_hbm, rim, pixels - rim, pixels)]
        else:
            spans = [(obs_hbm, 0, 0, pixels)]
        for src, origin, begin, end in spans:
            begin_n, end_n = max(begin, low), min(end, high)
            if begin_n < end_n:
                fetch(
                    src.at[:, pl.ds(origin + begin_n - begin, end_n - begin_n)],
                    obs.at[:, pl.ds(rim + begin_n, end_n - begin_n)],
                )
        if n == SEGMENTS - 1:
            fetch(bot_hbm.at[part, :], obs.at[:, pl.ds(rim + pixels, rim)])
    if last:
        waits.append([])
        fetch(smooth_hbm, smooth.at[pl.ds(0, own), :])
        fetch(factor_hbm, factor_ref)

    def start(n):
        for copy in waits[n] if n < len(waits) else []:
            copy.start()

    for n in range(AHEAD):
        start(n)
    s1 = jnp.concatenate([rows_ref[0:1, :]] * 2, axis=1)
    s2 = jnp.concatenate([rows_ref[1:2, :]] * 2, axis=1)
    inside_top = rows_ref[2:3, :]
    inside_bot = rows_ref[3:4, :]

    def departures(t):
        at = pl.multiple_of(t * wide, wide)
        here = prof[pl.ds(at, wide), :]
        terms = [
            lax.dot_general(jac_ref[m], here, (((1,), (1,)), ((), ())), preferred_element_type=jnp.float32)
            for m in range(3)
        ]
        field[:, pl.ds(at, wide)] = obs[:, pl.ds(at, wide)].astype(jnp.float32) - (
            terms[0] + s1 * terms[1] + s2 * terms[2]
        )

    def shifts(i, moved):
        rows = pl.ds(pl.multiple_of(i * 16, 16), 16)
        tiles = []
        for j in range(1, total - 1):
            here = field[rows, j * XTRACK : (j + 1) * XTRACK]
            high = here.astype(jnp.bfloat16)
            low = (here - high.astype(jnp.float32)).astype(jnp.bfloat16)
            tiles.append(jnp.concatenate([high, low], axis=1))
        moved[...] = jnp.dot(
            jnp.concatenate(tiles, axis=0), shift_ref[...], preferred_element_type=jnp.float32
        )

    def sweeps(i, moved):
        rows = pl.ds(pl.multiple_of(i * 16, 16), 16)
        chan = pl.ds(pl.multiple_of(first + i * 16, 16), 16)
        along = jnp.broadcast_to(rates_ref[rows, 0:1], (16, XTRACK))
        cross = jnp.broadcast_to(rates_ref[rows, 1:2], (16, XTRACK))
        stay = 1.0 - 2.0 * along - 2.0 * cross
        along, cross = along / stay, cross / stay
        cross = [3.0 * cross, 3.0 * cross * cross, cross * cross * cross]
        stay = stay * stay * stay
        fields = [{}, {}, {}, {}]
        for j in range(total):
            fields[0][j] = field[rows, j * XTRACK : (j + 1) * XTRACK]
            for k in range(1, HALO + 1):
                at = j - k
                if at < k:
                    continue
                prev = fields[k - 1]
                new = (
                    prev[at]
                    + along * (prev[at - 1] + prev[at + 1])
                    + cross[k - 1] * moved[(at - 1) * 16 : at * 16, (k - 1) * XTRACK : k * XTRACK]
                )
                if at < HALO:
                    new = new * inside_top
                if at >= HALO + lines:
                    new = new * inside_bot
                fields[k][at] = new
                del prev[at - 1]
                if k == HALO:
                    line = at - HALO
                    smooth[chan, line * XTRACK : (line + 1) * XTRACK] = (new * stay).astype(smooth.dtype)

    for n in range(SEGMENTS):
        for copy in waits[n]:
            copy.wait()
        start(n + AHEAD)
        pl.loop(cuts[n], cuts[n + 1], unroll=cuts[n + 1] - cuts[n])(departures)

    def smooth_copy(n, size):
        rows = pl.ds(pl.multiple_of(n, 16), size)
        return pltpu.make_async_copy(smooth.at[rows, :], out_hbm.at[rows, :], out_sems.at[0])

    shifts(0, moved_a)

    @pl.loop(0, groups // 2, unroll=groups // 2)
    def _(h):
        shifts(2 * h + 1, moved_b)
        sweeps(2 * h, moved_a)
        shifts(jnp.minimum(2 * h + 2, groups - 1), moved_a)
        sweeps(2 * h + 1, moved_b)
        if not last:
            smooth_copy(32 * h, 32).start()

    if groups % 2:
        sweeps(groups - 1, moved_a)
        if not last:
            smooth_copy(16 * (groups - 1), 16).start()

    if not last:
        smooth_copy(0, own).wait()
        return

    for copy in waits[SEGMENTS]:
        copy.wait()

    def out_copy(t):
        at = pl.multiple_of(t * OUT_BLOCK, OUT_BLOCK)
        return pltpu.make_async_copy(
            out.at[:, pl.ds(at, OUT_BLOCK)], out_hbm.at[:, pl.ds(at, OUT_BLOCK)], out_sems.at[t]
        )

    @pl.loop(0, pixels // OUT_BLOCK, unroll=pixels // OUT_BLOCK)
    def _(t):
        at = pl.multiple_of(t * OUT_BLOCK, OUT_BLOCK)
        out[:, pl.ds(at, OUT_BLOCK)] = jnp.dot(
            factor_ref[...], smooth[:, pl.ds(at, OUT_BLOCK)], preferred_element_type=jnp.float32
        )
        out_copy(t).start()

    pl.loop(0, pixels // OUT_BLOCK)(lambda t: out_copy(t).wait())


def half_call(last, anys, whole):
    own, pixels = anys[5].shape[1], anys[0].shape[0]
    rim = anys[1].shape[0]
    full = pixels + 2 * rim
    dtype = jnp.float32 if last else jnp.bfloat16
    scratch = [
        pltpu.VMEM((full, anys[0].shape[1]), jnp.bfloat16),
        pltpu.VMEM((own, full), jnp.bfloat16),
        pltpu.VMEM(anys[5].shape, jnp.bfloat16),
        pltpu.VMEM((own, full), jnp.float32),
        pltpu.VMEM((16 * (full // XTRACK - 2), HALO * XTRACK), jnp.float32),
        pltpu.VMEM((16 * (full // XTRACK - 2), HALO * XTRACK), jnp.float32),
        pltpu.VMEM((2 * own if last else own, pixels), jnp.bfloat16),
        pltpu.SemaphoreType.DMA((32,)),
        pltpu.SemaphoreType.DMA((pixels // OUT_BLOCK,)),
    ]
    if last:
        scratch += [pltpu.VMEM((own, pixels), jnp.float32), pltpu.VMEM((own, 2 * own), jnp.bfloat16)]
    return pl.pallas_call(
        functools.partial(half_kernel, last),
        out_shape=jax.ShapeDtypeStruct((own, pixels), dtype),
        in_specs=[pl.BlockSpec(memory_space=pl.ANY)] * len(anys)
        + [pl.BlockSpec(memory_space=pltpu.SMEM)]
        + [pl.BlockSpec(memory_space=pltpu.VMEM)] * (len(whole) - 1),
        out_specs=pl.BlockSpec(memory_space=pl.ANY),
        scratch_shapes=scratch,
        compiler_params=pltpu.CompilerParams(vmem_limit_bytes=LAST_LIMIT if last else OWN_LIMIT),
        name="other_half_and_factor" if last else "own_half",
    )(*anys, *whole)


def on_device_two(grid_profiles, send_lists, counts, angle_index, jacobian, observed, kappa, factor):
    own, pixels = observed.shape
    rim = HALO * XTRACK
    swath = lax.axis_size("swath")
    place = lax.axis_index("swath")
    half = lax.axis_index("chan")
    swap = [(0, 1), (1, 0)]
    forward = [(i, i + 1) for i in range(swath - 1)]
    backward = [(i + 1, i) for i in range(swath - 1)]

    jac_own = jnp.swapaxes(jacobian, 1, 2)
    jac_half = lax.dynamic_slice_in_dim(jac_own, (place % 2) * (own // 2), own // 2, axis=1)
    jac_near = lax.ppermute(jac_half, "chan", swap)
    rates_own = kappa.T
    rates_oth = lax.ppermute(rates_own, "chan", swap)
    outgoing = gather_rows(grid_profiles, send_lists[0], counts)
    outgoing, obs_late = lax.optimization_barrier((outgoing, observed))
    bnd_own = jnp.concatenate([obs_late[:, :rim], obs_late[:, pixels - rim :]], axis=1)
    bnd_oth = lax.ppermute(bnd_own, "chan", swap)
    incoming = lax.all_to_all(outgoing, "swath", split_axis=0, concat_axis=0, tiled=True)
    middle = obs_late[:, rim : pixels - rim]
    middle, bnd_oth = lax.optimization_barrier((middle, bnd_oth))
    mid_oth = lax.ppermute(middle, "chan", swap)
    jac_far = lax.ppermute(jac_near, "swath", [(i, i ^ 1) for i in range(swath)])
    jac_oth = jnp.where(
        place % 2 == 0,
        jnp.concatenate([jac_near, jac_far], axis=1),
        jnp.concatenate([jac_far, jac_near], axis=1),
    )
    near = np.eye(XTRACK, k=1) + np.eye(XTRACK, k=-1)
    moves = np.concatenate([near, near @ near, near @ near @ near], axis=1)
    shift = jnp.asarray(np.concatenate([moves, moves], axis=0), jnp.bfloat16)
    slant = slant_of(angle_index)
    ones = jnp.ones((XTRACK,), jnp.float32)
    rows = jnp.stack([
        slant,
        slant * slant,
        jnp.where(place > 0, ones, 0.0),
        jnp.where(place < swath - 1, ones, 0.0),
    ])
    factor_two = jnp.where(half == 0, factor, jnp.roll(factor, own, axis=1))

    bnd_own, bnd_oth, jac_oth, rates_oth, rows, factor_two = lax.optimization_barrier(
        (bnd_own, bnd_oth, jac_oth, rates_oth, rows, factor_two)
    )
    bnd_both = jnp.concatenate([bnd_own, bnd_oth], axis=0)
    obs_top = lax.ppermute(bnd_both[:, rim:], "swath", forward)
    obs_bot = lax.ppermute(bnd_both[:, :rim], "swath", backward)

    profiles = incoming.reshape(pixels, grid_profiles.shape[1])
    odd = place % 2
    head, tail = profiles[:rim], profiles[pixels - rim :]
    pairs = [(i, i ^ 1) for i in range(swath)]
    between = [(i, (i + 1 if i % 2 else i - 1)) for i in range(1, swath - 1)]
    prof_near = lax.ppermute(jnp.where(odd == 1, head, tail), "swath", pairs)
    prof_next = lax.ppermute(jnp.where(odd == 1, tail, head), "swath", between)
    odd = jnp.full((1,), odd, jnp.int32)

    smooth_own = half_call(
        False,
        (profiles, prof_near, prof_next, obs_top, obs_bot, jac_own, observed),
        (odd, rates_own, rows, shift),
    )
    return half_call(
        True,
        (profiles, prof_near, prof_next, obs_top, obs_bot, jac_oth, mid_oth, bnd_oth, smooth_own, factor_two),
        (odd, rates_oth, rows, shift),
    )


def solution(mesh):
    in_specs = (
        P("swath", None),
        P("swath", None, None),
        P("swath", None),
        P(),
        P(None, None, "chan"),
        P("chan", "swath"),
        P(None, "chan"),
        P("chan", None),
    )
    out_specs = P("chan", "swath")
    on_device = on_device_two if mesh.shape["chan"] == 2 else on_device_plain
    return jax.shard_map(
        on_device, mesh=mesh, in_specs=in_specs, out_specs=out_specs, check_vma=False
    )
```

```python
import functools
import math

import jax
import jax.numpy as jnp
import numpy as np
from jax import lax
from jax.experimental import pallas as pl
from jax.experimental.pallas import tpu as pltpu
from jax.sharding import PartitionSpec as P

XTRACK = 128
NANG = 8
HALO = 3
OUT_BLOCK = 512
GATHER_LIMIT = 60 * 1024 * 1024
OWN_LIMIT = 60 * 1024 * 1024
LAST_LIMIT = 60 * 1024 * 1024
SEGMENTS = 4
AHEAD = 2


max_zenith = math.pi / 3.0


def extended_2(block, sides, width):
    for axis, dim in sides:
        count = lax.axis_size(axis)
        forward = [(i, i + 1) for i in range(count - 1)]
        backward = [(target, source) for source, target in forward]
        low = lax.ppermute(
            lax.slice_in_dim(block, block.shape[dim] - width, None, axis=dim), axis, forward
        )
        high = lax.ppermute(lax.slice_in_dim(block, 0, width, axis=dim), axis, backward)
        block = jnp.concatenate([low, block, high], axis=dim)
    return block


def diffuse_once(extended, along_rate, cross_rate):
    center = extended[:, 1:-1]
    along_sum = extended[:, 2:] + extended[:, :-2] - 2.0 * center
    side_pad = jnp.pad(center, ((0, 0), (0, 0), (1, 1)))
    cross_sum = side_pad[:, :, 2:] + side_pad[:, :, :-2] - 2.0 * center
    return center + along_rate * along_sum + cross_rate * cross_sum


def line_rims(smooth_field):
    return extended_2(smooth_field, (("swath", 1),), 1)


def slant_of(angle_index):
    zenith = angle_index.astype(jnp.float32) * (max_zenith / (NANG - 1))
    return 1.0 / jnp.cos(zenith) - 1.0


def on_device_plain(grid_profiles, send_lists, counts, angle_index, jacobian, observed, kappa, factor):
    slot_rows = send_lists[0]
    slots = slot_rows.shape[1]
    own_chan = observed.shape[0]
    pixel_count = observed.shape[1]
    line_count = pixel_count // XTRACK
    live_slot = jnp.arange(slots, dtype=jnp.int32)[None, :] < counts[0][:, None]
    zero_value = jnp.zeros((), grid_profiles.dtype)
    outgoing = jnp.where(live_slot[:, :, None], grid_profiles[slot_rows], zero_value)
    incoming = lax.all_to_all(outgoing, "swath", split_axis=0, concat_axis=0, tiled=True)
    pixel_profiles = incoming.reshape(pixel_count, grid_profiles.shape[1])
    model = jnp.einsum("mkc,pk->mcp", jacobian, pixel_profiles, preferred_element_type=jnp.float32)
    slant_path = slant_of(angle_index)
    model = model.reshape(3, own_chan, line_count, XTRACK)
    departure = observed.astype(jnp.float32).reshape(own_chan, line_count, XTRACK) - (
        model[0] + slant_path * model[1] + slant_path * slant_path * model[2]
    )
    along_rate = kappa[0][:, None, None]
    cross_rate = kappa[1][:, None, None]
    smooth_field = departure
    for sweep in range(3):
        smooth_field = diffuse_once(line_rims(smooth_field), along_rate, cross_rate)
    smoothed = smooth_field.reshape(own_chan, pixel_count).astype(jnp.bfloat16)
    return jnp.dot(
        factor,
        lax.all_gather(smoothed, "chan", axis=0, tiled=True),
        preferred_element_type=jnp.float32,
    )


def gather_kernel(lists_hbm, counts_hbm, grid_hbm, out_hbm, lists, counts, grid, out, sems, out_sem):
    ins = [(lists_hbm, lists), (counts_hbm, counts), (grid_hbm, grid)]
    ins = [pltpu.make_async_copy(src, dst, sems.at[n]) for n, (src, dst) in enumerate(ins)]
    for copy in ins:
        copy.start()
    for copy in ins[:2]:
        copy.wait()
    grid_rows = grid.shape[0]
    parts, slots = lists.shape
    slot_number = lax.broadcasted_iota(jnp.int32, (slots, parts), 0)
    picks = jnp.where(slot_number < counts[...], lists[...].T, -1)
    row_number = lax.broadcasted_iota(jnp.int32, (slots, grid_rows), 1)
    ins[2].wait()
    for part in range(parts):
        one_hot = (picks[:, part : part + 1] == row_number).astype(jnp.float32).astype(jnp.bfloat16)
        rows = jnp.dot(one_hot, grid[...], preferred_element_type=jnp.float32)
        out[part] = rows.astype(out.dtype)
        pltpu.make_async_copy(out.at[part], out_hbm.at[part], out_sem).start()
    pltpu.make_async_copy(out, out_hbm, out_sem).wait()


def gather_rows(grid_profiles, slot_rows, counts):
    parts, slots = slot_rows.shape
    shape = (parts, slots, grid_profiles.shape[1])
    return pl.pallas_call(
        gather_kernel,
        out_shape=jax.ShapeDtypeStruct(shape, grid_profiles.dtype),
        in_specs=[pl.BlockSpec(memory_space=pl.ANY)] * 3,
        out_specs=pl.BlockSpec(memory_space=pl.ANY),
        scratch_shapes=[
            pltpu.VMEM(slot_rows.shape, jnp.int32),
            pltpu.VMEM(counts.shape, jnp.int32),
            pltpu.VMEM(grid_profiles.shape, grid_profiles.dtype),
            pltpu.VMEM(shape, grid_profiles.dtype),
            pltpu.SemaphoreType.DMA((3,)),
            pltpu.SemaphoreType.DMA,
        ],
        compiler_params=pltpu.CompilerParams(vmem_limit_bytes=GATHER_LIMIT),
        name="pick_rows",
    )(slot_rows, counts, grid_profiles)


def half_kernel(last, *refs):
    prof_hbm, prof_near_hbm, prof_next_hbm, top_hbm, bot_hbm, jac_hbm = refs[:6]
    if last:
        mid_hbm, bnd_hbm, smooth_hbm, factor_hbm, rates_hbm, rows_hbm, shift_hbm = refs[6:13]
        out_hbm, *refs, out, factor_ref = refs[13:]
    else:
        obs_hbm, rates_hbm, rows_hbm, shift_hbm = refs[6:10]
        out_hbm, *refs = refs[10:]
    prof, obs, jac_ref, field, moved_a, moved_b, smooth, rates_ref, rows_ref, shift_ref, sems, out_sems = refs
    own, pixels = jac_hbm.shape[1], prof_hbm.shape[0]
    odd = lax.rem(lax.axis_index("swath"), 2)
    rim = prof_near_hbm.shape[0]
    lines = pixels // XTRACK
    wide = 2 * XTRACK
    full = pixels + 2 * rim
    total = full // XTRACK
    first = own if last else 0
    groups = own // 16

    blocks = full // wide
    cuts = [blocks * n // SEGMENTS for n in range(SEGMENTS + 1)]
    part = pl.ds(first, own)
    waits = []
    copies = []

    def fetch(src, dst):
        copy = pltpu.make_async_copy(src, dst, sems.at[len(copies)])
        copies.append(copy)
        waits[-1].append(copy)

    for n in range(SEGMENTS):
        waits.append([])
        if n == 0:
            fetch(jac_hbm, jac_ref)
            fetch(rows_hbm, rows_ref)
            fetch(rates_hbm, rates_ref)
            fetch(shift_hbm, shift_ref)
            for src, number in ((prof_near_hbm, 1 - odd), (prof_next_hbm, odd)):
                fetch(src, prof.at[pl.ds(pl.multiple_of(number * (rim + pixels), XTRACK), rim), :])
            fetch(top_hbm.at[part, :], obs.at[:, pl.ds(0, rim)])
        low = max(cuts[n] * wide - rim, 0)
        high = min(cuts[n + 1] * wide - rim, pixels)
        fetch(prof_hbm.at[pl.ds(low, high - low), :], prof.at[pl.ds(rim + low, high - low), :])
        if last:
            spans = [(bnd_hbm, 0, 0, rim), (mid_hbm, 0, rim, pixels - rim), (bnd_hbm, rim, pixels - rim, pixels)]
        else:
            spans = [(obs_hbm, 0, 0, pixels)]
        for src, origin, begin, end in spans:
            begin_n, end_n = max(begin, low), min(end, high)
            if begin_n < end_n:
                fetch(
                    src.at[:, pl.ds(origin + begin_n - begin, end_n - begin_n)],
                    obs.at[:, pl.ds(rim + begin_n, end_n - begin_n)],
                )
        if n == SEGMENTS - 1:
            fetch(bot_hbm.at[part, :], obs.at[:, pl.ds(rim + pixels, rim)])
    if last:
        waits.append([])
        fetch(smooth_hbm, smooth.at[pl.ds(0, own), :])
        fetch(factor_hbm, factor_ref)

    def start(n):
        for copy in waits[n] if n < len(waits) else []:
            copy.start()

    for n in range(AHEAD):
        start(n)
    for copy in waits[0]:
        copy.wait()
    s1 = jnp.concatenate([rows_ref[0:1, :]] * 2, axis=1)
    s2 = jnp.concatenate([rows_ref[1:2, :]] * 2, axis=1)
    inside_top = rows_ref[2:3, :]
    inside_bot = rows_ref[3:4, :]

    def departures(t):
        at = pl.multiple_of(t * wide, wide)
        here = prof[pl.ds(at, wide), :]
        terms = [
            lax.dot_general(jac_ref[m], here, (((1,), (1,)), ((), ())), preferred_element_type=jnp.float32)
            for m in range(3)
        ]
        field[:, pl.ds(at, wide)] = obs[:, pl.ds(at, wide)].astype(jnp.float32) - (
            terms[0] + s1 * terms[1] + s2 * terms[2]
        )

    def shifts(i, moved):
        rows = pl.ds(pl.multiple_of(i * 16, 16), 16)
        tiles = []
        for j in range(1, total - 1):
            here = field[rows, j * XTRACK : (j + 1) * XTRACK]
            high = here.astype(jnp.bfloat16)
            low = (here - high.astype(jnp.float32)).astype(jnp.bfloat16)
            tiles.append(jnp.concatenate([high, low], axis=1))
        moved[...] = jnp.dot(
            jnp.concatenate(tiles, axis=0), shift_ref[...], preferred_element_type=jnp.float32
        )

    def sweeps(i, moved):
        rows = pl.ds(pl.multiple_of(i * 16, 16), 16)
        chan = pl.ds(pl.multiple_of(first + i * 16, 16), 16)
        along = jnp.broadcast_to(rates_ref[rows, 0:1], (16, XTRACK))
        cross = jnp.broadcast_to(rates_ref[rows, 1:2], (16, XTRACK))
        stay = 1.0 - 2.0 * along - 2.0 * cross
        along, cross = along / stay, cross / stay
        cross = [3.0 * cross, 3.0 * cross * cross, cross * cross * cross]
        stay = stay * stay * stay
        fields = [{}, {}, {}, {}]
        for j in range(total):
            fields[0][j] = field[rows, j * XTRACK : (j + 1) * XTRACK]
            for k in range(1, HALO + 1):
                at = j - k
                if at < k:
                    continue
                prev = fields[k - 1]
                new = (
                    prev[at]
                    + along * (prev[at - 1] + prev[at + 1])
                    + cross[k - 1] * moved[(at - 1) * 16 : at * 16, (k - 1) * XTRACK : k * XTRACK]
                )
                if at < HALO:
                    new = new * inside_top
                if at >= HALO + lines:
                    new = new * inside_bot
                fields[k][at] = new
                del prev[at - 1]
                if k == HALO:
                    line = at - HALO
                    smooth[chan, line * XTRACK : (line + 1) * XTRACK] = (new * stay).astype(smooth.dtype)

    for n in range(SEGMENTS):
        for copy in waits[n] if n else []:
            copy.wait()
        start(n + AHEAD)
        pl.loop(cuts[n], cuts[n + 1], unroll=cuts[n + 1] - cuts[n])(departures)

    def smooth_copy(n, size):
        rows = pl.ds(pl.multiple_of(n, 16), size)
        return pltpu.make_async_copy(smooth.at[rows, :], out_hbm.at[rows, :], out_sems.at[0])

    shifts(0, moved_a)

    @pl.loop(0, groups // 2, unroll=groups // 2)
    def _(h):
        shifts(2 * h + 1, moved_b)
        sweeps(2 * h, moved_a)
        shifts(jnp.minimum(2 * h + 2, groups - 1), moved_a)
        sweeps(2 * h + 1, moved_b)
        if not last:
            smooth_copy(32 * h, 32).start()

    if groups % 2:
        sweeps(groups - 1, moved_a)
        if not last:
            smooth_copy(16 * (groups - 1), 16).start()

    if not last:
        smooth_copy(0, own).wait()
        return

    for copy in waits[SEGMENTS]:
        copy.wait()

    def out_copy(t):
        at = pl.multiple_of(t * OUT_BLOCK, OUT_BLOCK)
        return pltpu.make_async_copy(
            out.at[:, pl.ds(at, OUT_BLOCK)], out_hbm.at[:, pl.ds(at, OUT_BLOCK)], out_sems.at[t]
        )

    @pl.loop(0, pixels // OUT_BLOCK, unroll=pixels // OUT_BLOCK)
    def _(t):
        at = pl.multiple_of(t * OUT_BLOCK, OUT_BLOCK)
        out[:, pl.ds(at, OUT_BLOCK)] = jnp.dot(
            factor_ref[...], smooth[:, pl.ds(at, OUT_BLOCK)], preferred_element_type=jnp.float32
        )
        out_copy(t).start()

    pl.loop(0, pixels // OUT_BLOCK)(lambda t: out_copy(t).wait())


def half_call(last, anys, small):
    own, pixels = anys[5].shape[1], anys[0].shape[0]
    rim = anys[1].shape[0]
    full = pixels + 2 * rim
    dtype = jnp.float32 if last else jnp.bfloat16
    scratch = [
        pltpu.VMEM((full, anys[0].shape[1]), jnp.bfloat16),
        pltpu.VMEM((own, full), jnp.bfloat16),
        pltpu.VMEM(anys[5].shape, jnp.bfloat16),
        pltpu.VMEM((own, full), jnp.float32),
        pltpu.VMEM((16 * (full // XTRACK - 2), HALO * XTRACK), jnp.float32),
        pltpu.VMEM((16 * (full // XTRACK - 2), HALO * XTRACK), jnp.float32),
        pltpu.VMEM((2 * own if last else own, pixels), jnp.bfloat16),
        *[pltpu.VMEM(x.shape, x.dtype) for x in small],
        pltpu.SemaphoreType.DMA((32,)),
        pltpu.SemaphoreType.DMA((pixels // OUT_BLOCK,)),
    ]
    if last:
        scratch += [pltpu.VMEM((own, pixels), jnp.float32), pltpu.VMEM((own, 2 * own), jnp.bfloat16)]
    return pl.pallas_call(
        functools.partial(half_kernel, last),
        out_shape=jax.ShapeDtypeStruct((own, pixels), dtype),
        in_specs=[pl.BlockSpec(memory_space=pl.ANY)] * (len(anys) + len(small)),
        out_specs=pl.BlockSpec(memory_space=pl.ANY),
        scratch_shapes=scratch,
        compiler_params=pltpu.CompilerParams(vmem_limit_bytes=LAST_LIMIT if last else OWN_LIMIT),
        name="other_half_and_factor" if last else "own_half",
    )(*anys, *small)


def on_device_two(grid_profiles, send_lists, counts, angle_index, jacobian, observed, kappa, factor):
    own, pixels = observed.shape
    rim = HALO * XTRACK
    swath = lax.axis_size("swath")
    place = lax.axis_index("swath")
    half = lax.axis_index("chan")
    swap = [(0, 1), (1, 0)]
    forward = [(i, i + 1) for i in range(swath - 1)]
    backward = [(i + 1, i) for i in range(swath - 1)]

    jac_own = jnp.swapaxes(jacobian, 1, 2)
    jac_half = lax.dynamic_slice_in_dim(jac_own, (place % 2) * (own // 2), own // 2, axis=1)
    jac_near = lax.ppermute(jac_half, "chan", swap)
    rates_own = kappa.T
    rates_oth = lax.ppermute(rates_own, "chan", swap)
    outgoing = gather_rows(grid_profiles, send_lists[0], counts)
    outgoing, obs_late = lax.optimization_barrier((outgoing, observed))
    bnd_own = jnp.concatenate([obs_late[:, :rim], obs_late[:, pixels - rim :]], axis=1)
    bnd_oth = lax.ppermute(bnd_own, "chan", swap)
    incoming = lax.all_to_all(outgoing, "swath", split_axis=0, concat_axis=0, tiled=True)
    middle = obs_late[:, rim : pixels - rim]
    middle, bnd_oth = lax.optimization_barrier((middle, bnd_oth))
    mid_oth = lax.ppermute(middle, "chan", swap)
    jac_far = lax.ppermute(jac_near, "swath", [(i, i ^ 1) for i in range(swath)])
    jac_oth = jnp.where(
        place % 2 == 0,
        jnp.concatenate([jac_near, jac_far], axis=1),
        jnp.concatenate([jac_far, jac_near], axis=1),
    )
    near = np.eye(XTRACK, k=1) + np.eye(XTRACK, k=-1)
    moves = np.concatenate([near, near @ near, near @ near @ near], axis=1)
    shift = jnp.asarray(np.concatenate([moves, moves], axis=0), jnp.bfloat16)
    slant = slant_of(angle_index)
    ones = jnp.ones((XTRACK,), jnp.float32)
    rows = jnp.stack([
        slant,
        slant * slant,
        jnp.where(place > 0, ones, 0.0),
        jnp.where(place < swath - 1, ones, 0.0),
    ])
    factor_two = jnp.where(half == 0, factor, jnp.roll(factor, own, axis=1))

    bnd_own, bnd_oth, jac_oth, rates_oth, rows, factor_two = lax.optimization_barrier(
        (bnd_own, bnd_oth, jac_oth, rates_oth, rows, factor_two)
    )
    bnd_both = jnp.concatenate([bnd_own, bnd_oth], axis=0)
    obs_top = lax.ppermute(bnd_both[:, rim:], "swath", forward)
    obs_bot = lax.ppermute(bnd_both[:, :rim], "swath", backward)

    profiles = incoming.reshape(pixels, grid_profiles.shape[1])
    odd = place % 2
    head, tail = profiles[:rim], profiles[pixels - rim :]
    pairs = [(i, i ^ 1) for i in range(swath)]
    between = [(i, (i + 1 if i % 2 else i - 1)) for i in range(1, swath - 1)]
    prof_near = lax.ppermute(jnp.where(odd == 1, head, tail), "swath", pairs)
    prof_next = lax.ppermute(jnp.where(odd == 1, tail, head), "swath", between)

    smooth_own = half_call(
        False,
        (profiles, prof_near, prof_next, obs_top, obs_bot, jac_own, observed),
        (rates_own, rows, shift),
    )
    return half_call(
        True,
        (profiles, prof_near, prof_next, obs_top, obs_bot, jac_oth, mid_oth, bnd_oth, smooth_own, factor_two),
        (rates_oth, rows, shift),
    )


def solution(mesh):
    in_specs = (
        P("swath", None),
        P("swath", None, None),
        P("swath", None),
        P(),
        P(None, None, "chan"),
        P("chan", "swath"),
        P(None, "chan"),
        P("chan", None),
    )
    out_specs = P("chan", "swath")
    on_device = on_device_two if mesh.shape["chan"] == 2 else on_device_plain
    return jax.shard_map(
        on_device, mesh=mesh, in_specs=in_specs, out_specs=out_specs, check_vma=False
    )
```

```python
import functools
import math

import jax
import jax.numpy as jnp
import numpy as np
from jax import lax
from jax.experimental import pallas as pl
from jax.experimental.pallas import tpu as pltpu
from jax.sharding import PartitionSpec as P

XTRACK = 128
NANG = 8
HALO = 3
OUT_BLOCK = 512
GATHER_LIMIT = 60 * 1024 * 1024
OWN_LIMIT = 60 * 1024 * 1024
LAST_LIMIT = 60 * 1024 * 1024
SEGMENTS = 4
AHEAD = 2


max_zenith = math.pi / 3.0


def extended_2(block, sides, width):
    for axis, dim in sides:
        count = lax.axis_size(axis)
        forward = [(i, i + 1) for i in range(count - 1)]
        backward = [(target, source) for source, target in forward]
        low = lax.ppermute(
            lax.slice_in_dim(block, block.shape[dim] - width, None, axis=dim), axis, forward
        )
        high = lax.ppermute(lax.slice_in_dim(block, 0, width, axis=dim), axis, backward)
        block = jnp.concatenate([low, block, high], axis=dim)
    return block


def diffuse_once(extended, along_rate, cross_rate):
    center = extended[:, 1:-1]
    along_sum = extended[:, 2:] + extended[:, :-2] - 2.0 * center
    side_pad = jnp.pad(center, ((0, 0), (0, 0), (1, 1)))
    cross_sum = side_pad[:, :, 2:] + side_pad[:, :, :-2] - 2.0 * center
    return center + along_rate * along_sum + cross_rate * cross_sum


def line_rims(smooth_field):
    return extended_2(smooth_field, (("swath", 1),), 1)


def slant_of(angle_index):
    zenith = angle_index.astype(jnp.float32) * (max_zenith / (NANG - 1))
    return 1.0 / jnp.cos(zenith) - 1.0


def on_device_plain(grid_profiles, send_lists, counts, angle_index, jacobian, observed, kappa, factor):
    slot_rows = send_lists[0]
    slots = slot_rows.shape[1]
    own_chan = observed.shape[0]
    pixel_count = observed.shape[1]
    line_count = pixel_count // XTRACK
    live_slot = jnp.arange(slots, dtype=jnp.int32)[None, :] < counts[0][:, None]
    zero_value = jnp.zeros((), grid_profiles.dtype)
    outgoing = jnp.where(live_slot[:, :, None], grid_profiles[slot_rows], zero_value)
    incoming = lax.all_to_all(outgoing, "swath", split_axis=0, concat_axis=0, tiled=True)
    pixel_profiles = incoming.reshape(pixel_count, grid_profiles.shape[1])
    model = jnp.einsum("mkc,pk->mcp", jacobian, pixel_profiles, preferred_element_type=jnp.float32)
    slant_path = slant_of(angle_index)
    model = model.reshape(3, own_chan, line_count, XTRACK)
    departure = observed.astype(jnp.float32).reshape(own_chan, line_count, XTRACK) - (
        model[0] + slant_path * model[1] + slant_path * slant_path * model[2]
    )
    along_rate = kappa[0][:, None, None]
    cross_rate = kappa[1][:, None, None]
    smooth_field = departure
    for sweep in range(3):
        smooth_field = diffuse_once(line_rims(smooth_field), along_rate, cross_rate)
    smoothed = smooth_field.reshape(own_chan, pixel_count).astype(jnp.bfloat16)
    return jnp.dot(
        factor,
        lax.all_gather(smoothed, "chan", axis=0, tiled=True),
        preferred_element_type=jnp.float32,
    )


def gather_kernel(lists_hbm, counts_hbm, grid_hbm, out_hbm, lists, counts, grid, out, sems, out_sem):
    ins = [(lists_hbm, lists), (counts_hbm, counts), (grid_hbm, grid)]
    ins = [pltpu.make_async_copy(src, dst, sems.at[n]) for n, (src, dst) in enumerate(ins)]
    for copy in ins:
        copy.start()
    for copy in ins[:2]:
        copy.wait()
    grid_rows = grid.shape[0]
    parts, slots = lists.shape
    slot_number = lax.broadcasted_iota(jnp.int32, (slots, parts), 0)
    picks = jnp.where(slot_number < counts[...], lists[...].T, -1)
    row_number = lax.broadcasted_iota(jnp.int32, (slots, grid_rows), 1)
    ins[2].wait()
    for part in range(parts):
        one_hot = (picks[:, part : part + 1] == row_number).astype(jnp.float32).astype(jnp.bfloat16)
        rows = jnp.dot(one_hot, grid[...], preferred_element_type=jnp.float32)
        out[part] = rows.astype(out.dtype)
        pltpu.make_async_copy(out.at[part], out_hbm.at[part], out_sem).start()
    pltpu.make_async_copy(out, out_hbm, out_sem).wait()


def gather_rows(grid_profiles, slot_rows, counts):
    parts, slots = slot_rows.shape
    shape = (parts, slots, grid_profiles.shape[1])
    return pl.pallas_call(
        gather_kernel,
        out_shape=jax.ShapeDtypeStruct(shape, grid_profiles.dtype),
        in_specs=[pl.BlockSpec(memory_space=pl.ANY)] * 3,
        out_specs=pl.BlockSpec(memory_space=pl.ANY),
        scratch_shapes=[
            pltpu.VMEM(slot_rows.shape, jnp.int32),
            pltpu.VMEM(counts.shape, jnp.int32),
            pltpu.VMEM(grid_profiles.shape, grid_profiles.dtype),
            pltpu.VMEM(shape, grid_profiles.dtype),
            pltpu.SemaphoreType.DMA((3,)),
            pltpu.SemaphoreType.DMA,
        ],
        compiler_params=pltpu.CompilerParams(vmem_limit_bytes=GATHER_LIMIT),
        name="pick_rows",
    )(slot_rows, counts, grid_profiles)


def half_kernel(last, *refs):
    prof_hbm, prof_near_hbm, prof_next_hbm, top_hbm, bot_hbm, jac_hbm = refs[:6]
    if last:
        mid_hbm, bnd_hbm, smooth_hbm, factor_hbm, rates_hbm, rows_hbm, shift_hbm = refs[6:13]
        out_hbm, *refs, out, factor_ref = refs[13:]
    else:
        obs_hbm, rates_hbm, rows_hbm, shift_hbm = refs[6:10]
        out_hbm, *refs = refs[10:]
    prof, obs, jac_ref, field, moved_a, moved_b, smooth, rates_ref, rows_ref, shift_ref, sems, out_sems = refs
    own, pixels = jac_hbm.shape[1], prof_hbm.shape[0]
    odd = lax.rem(lax.axis_index("swath"), 2)
    rim = prof_near_hbm.shape[0]
    lines = pixels // XTRACK
    wide = 2 * XTRACK
    full = pixels + 2 * rim
    total = full // XTRACK
    first = own if last else 0
    groups = own // 16

    blocks = full // wide
    cuts = [blocks * n // SEGMENTS for n in range(SEGMENTS + 1)]
    part = pl.ds(first, own)
    waits = []
    copies = []

    def fetch(src, dst):
        copy = pltpu.make_async_copy(src, dst, sems.at[len(copies)])
        copies.append(copy)
        waits[-1].append(copy)

    for n in range(SEGMENTS):
        waits.append([])
        if n == 0:
            fetch(jac_hbm, jac_ref)
            fetch(rows_hbm, rows_ref)
            fetch(rates_hbm, rates_ref)
            fetch(shift_hbm, shift_ref)
            for src, number in ((prof_near_hbm, 1 - odd), (prof_next_hbm, odd)):
                fetch(src, prof.at[pl.ds(pl.multiple_of(number * (rim + pixels), XTRACK), rim), :])
            fetch(top_hbm.at[part, :], obs.at[:, pl.ds(0, rim)])
        low = max(cuts[n] * wide - rim, 0)
        high = min(cuts[n + 1] * wide - rim, pixels)
        fetch(prof_hbm.at[pl.ds(low, high - low), :], prof.at[pl.ds(rim + low, high - low), :])
        if last:
            spans = [(bnd_hbm, 0, 0, rim), (mid_hbm, 0, rim, pixels - rim), (bnd_hbm, rim, pixels - rim, pixels)]
        else:
            spans = [(obs_hbm, 0, 0, pixels)]
        for src, origin, begin, end in spans:
            begin_n, end_n = max(begin, low), min(end, high)
            if begin_n < end_n:
                fetch(
                    src.at[:, pl.ds(origin + begin_n - begin, end_n - begin_n)],
                    obs.at[:, pl.ds(rim + begin_n, end_n - begin_n)],
                )
        if n == SEGMENTS - 1:
            fetch(bot_hbm.at[part, :], obs.at[:, pl.ds(rim + pixels, rim)])
    if last:
        waits.append([])
        fetch(smooth_hbm, smooth.at[pl.ds(0, own), :])
        fetch(factor_hbm, factor_ref)

    def start(n):
        for copy in waits[n] if n < len(waits) else []:
            copy.start()

    for n in range(AHEAD):
        start(n)
    for copy in waits[0]:
        copy.wait()
    s1 = jnp.concatenate([rows_ref[0:1, :]] * 2, axis=1)
    s2 = jnp.concatenate([rows_ref[1:2, :]] * 2, axis=1)
    inside_top = rows_ref[2:3, :]
    inside_bot = rows_ref[3:4, :]

    def departures(t):
        at = pl.multiple_of(t * wide, wide)
        here = prof[pl.ds(at, wide), :]
        terms = [
            lax.dot_general(jac_ref[m], here, (((1,), (1,)), ((), ())), preferred_element_type=jnp.float32)
            for m in range(3)
        ]
        field[:, pl.ds(at, wide)] = obs[:, pl.ds(at, wide)].astype(jnp.float32) - (
            terms[0] + s1 * terms[1] + s2 * terms[2]
        )

    def shifts(i, moved):
        rows = pl.ds(pl.multiple_of(i * 16, 16), 16)
        tiles = []
        for j in range(1, total - 1):
            here = field[rows, j * XTRACK : (j + 1) * XTRACK]
            high = here.astype(jnp.bfloat16)
            low = (here - high.astype(jnp.float32)).astype(jnp.bfloat16)
            tiles.append(jnp.concatenate([high, low], axis=1))
        moved[...] = jnp.dot(
            jnp.concatenate(tiles, axis=0), shift_ref[...], preferred_element_type=jnp.float32
        )

    def sweeps(i, moved):
        rows = pl.ds(pl.multiple_of(i * 16, 16), 16)
        chan = pl.ds(pl.multiple_of(first + i * 16, 16), 16)
        along = jnp.broadcast_to(rates_ref[rows, 0:1], (16, XTRACK))
        cross = jnp.broadcast_to(rates_ref[rows, 1:2], (16, XTRACK))
        stay = 1.0 - 2.0 * along - 2.0 * cross
        along, cross = along / stay, cross / stay
        cross = [3.0 * cross, 3.0 * cross * cross, cross * cross * cross]
        stay = stay * stay * stay
        fields = [{}, {}, {}, {}]
        for j in range(total):
            fields[0][j] = field[rows, j * XTRACK : (j + 1) * XTRACK]
            for k in range(1, HALO + 1):
                at = j - k
                if at < k:
                    continue
                prev = fields[k - 1]
                new = (
                    prev[at]
                    + along * (prev[at - 1] + prev[at + 1])
                    + cross[k - 1] * moved[(at - 1) * 16 : at * 16, (k - 1) * XTRACK : k * XTRACK]
                )
                if at < HALO:
                    new = new * inside_top
                if at >= HALO + lines:
                    new = new * inside_bot
                fields[k][at] = new
                del prev[at - 1]
                if k == HALO:
                    line = at - HALO
                    smooth[chan, line * XTRACK : (line + 1) * XTRACK] = (new * stay).astype(smooth.dtype)

    for n in range(SEGMENTS):
        for copy in waits[n] if n else []:
            copy.wait()
        start(n + AHEAD)
        pl.loop(cuts[n], cuts[n + 1], unroll=cuts[n + 1] - cuts[n])(departures)

    def smooth_copy(n, size):
        rows = pl.ds(pl.multiple_of(n, 16), size)
        return pltpu.make_async_copy(smooth.at[rows, :], out_hbm.at[rows, :], out_sems.at[0])

    shifts(0, moved_a)

    @pl.loop(0, groups // 2, unroll=groups // 2)
    def _(h):
        shifts(2 * h + 1, moved_b)
        sweeps(2 * h, moved_a)
        shifts(jnp.minimum(2 * h + 2, groups - 1), moved_a)
        sweeps(2 * h + 1, moved_b)
        if not last:
            smooth_copy(32 * h, 32).start()

    if groups % 2:
        sweeps(groups - 1, moved_a)
        if not last:
            smooth_copy(16 * (groups - 1), 16).start()

    if not last:
        smooth_copy(0, own).wait()
        return

    for copy in waits[SEGMENTS]:
        copy.wait()

    def out_copy(t):
        at = pl.multiple_of(t * OUT_BLOCK, OUT_BLOCK)
        return pltpu.make_async_copy(
            out.at[:, pl.ds(at, OUT_BLOCK)], out_hbm.at[:, pl.ds(at, OUT_BLOCK)], out_sems.at[t]
        )

    @pl.loop(0, pixels // OUT_BLOCK, unroll=pixels // OUT_BLOCK)
    def _(t):
        at = pl.multiple_of(t * OUT_BLOCK, OUT_BLOCK)
        out[:, pl.ds(at, OUT_BLOCK)] = jnp.dot(
            factor_ref[...], smooth[:, pl.ds(at, OUT_BLOCK)], preferred_element_type=jnp.float32
        )
        out_copy(t).start()

    pl.loop(0, pixels // OUT_BLOCK)(lambda t: out_copy(t).wait())


def half_call(last, anys, small):
    own, pixels = anys[5].shape[1], anys[0].shape[0]
    rim = anys[1].shape[0]
    full = pixels + 2 * rim
    dtype = jnp.float32 if last else jnp.bfloat16
    scratch = [
        pltpu.VMEM((full, anys[0].shape[1]), jnp.bfloat16),
        pltpu.VMEM((own, full), jnp.bfloat16),
        pltpu.VMEM(anys[5].shape, jnp.bfloat16),
        pltpu.VMEM((own, full), jnp.float32),
        pltpu.VMEM((16 * (full // XTRACK - 2), HALO * XTRACK), jnp.float32),
        pltpu.VMEM((16 * (full // XTRACK - 2), HALO * XTRACK), jnp.float32),
        pltpu.VMEM((2 * own if last else own, pixels), jnp.bfloat16),
        *[pltpu.VMEM(x.shape, x.dtype) for x in small],
        pltpu.SemaphoreType.DMA((32,)),
        pltpu.SemaphoreType.DMA((pixels // OUT_BLOCK,)),
    ]
    if last:
        scratch += [pltpu.VMEM((own, pixels), jnp.float32), pltpu.VMEM((own, 2 * own), jnp.bfloat16)]
    return pl.pallas_call(
        functools.partial(half_kernel, last),
        out_shape=jax.ShapeDtypeStruct((own, pixels), dtype),
        in_specs=[pl.BlockSpec(memory_space=pl.ANY)] * (len(anys) + len(small)),
        out_specs=pl.BlockSpec(memory_space=pl.ANY),
        scratch_shapes=scratch,
        compiler_params=pltpu.CompilerParams(vmem_limit_bytes=LAST_LIMIT if last else OWN_LIMIT),
        name="other_half_and_factor" if last else "own_half",
    )(*anys, *small)


def on_device_two(grid_profiles, send_lists, counts, angle_index, jacobian, observed, kappa, factor):
    own, pixels = observed.shape
    rim = HALO * XTRACK
    swath = lax.axis_size("swath")
    place = lax.axis_index("swath")
    half = lax.axis_index("chan")
    swap = [(0, 1), (1, 0)]
    forward = [(i, i + 1) for i in range(swath - 1)]
    backward = [(i + 1, i) for i in range(swath - 1)]

    jac_own = jnp.swapaxes(jacobian, 1, 2)
    quarter = own // 4
    jac_part = lax.dynamic_slice_in_dim(jac_own, (place % 4) * quarter, quarter, axis=1)
    jac_near = lax.ppermute(jac_part, "chan", swap)
    rates_own = kappa.T
    rates_oth = lax.ppermute(rates_own, "chan", swap)
    outgoing = gather_rows(grid_profiles, send_lists[0], counts)
    outgoing, obs_late = lax.optimization_barrier((outgoing, observed))
    bnd_own = jnp.concatenate([obs_late[:, :rim], obs_late[:, pixels - rim :]], axis=1)
    bnd_oth = lax.ppermute(bnd_own, "chan", swap)
    incoming = lax.all_to_all(outgoing, "swath", split_axis=0, concat_axis=0, tiled=True)
    middle = obs_late[:, rim : pixels - rim]
    middle, bnd_oth = lax.optimization_barrier((middle, bnd_oth))
    mid_oth = lax.ppermute(middle, "chan", swap)
    jac_oth = jac_near
    for step in (1, 2):
        jac_far = lax.ppermute(jac_oth, "swath", [(i, i ^ step) for i in range(swath)])
        jac_oth = jnp.where(
            place // step % 2 == 0,
            jnp.concatenate([jac_oth, jac_far], axis=1),
            jnp.concatenate([jac_far, jac_oth], axis=1),
        )
    near = np.eye(XTRACK, k=1) + np.eye(XTRACK, k=-1)
    moves = np.concatenate([near, near @ near, near @ near @ near], axis=1)
    shift = jnp.asarray(np.concatenate([moves, moves], axis=0), jnp.bfloat16)
    slant = slant_of(angle_index)
    ones = jnp.ones((XTRACK,), jnp.float32)
    rows = jnp.stack([
        slant,
        slant * slant,
        jnp.where(place > 0, ones, 0.0),
        jnp.where(place < swath - 1, ones, 0.0),
    ])
    factor_two = jnp.where(half == 0, factor, jnp.roll(factor, own, axis=1))

    bnd_own, bnd_oth, rates_oth, rows, factor_two = lax.optimization_barrier(
        (bnd_own, bnd_oth, rates_oth, rows, factor_two)
    )
    bnd_both = jnp.concatenate([bnd_own, bnd_oth], axis=0)
    obs_top = lax.ppermute(bnd_both[:, rim:], "swath", forward)
    obs_bot = lax.ppermute(bnd_both[:, :rim], "swath", backward)

    profiles = incoming.reshape(pixels, grid_profiles.shape[1])
    profiles, jac_oth = lax.optimization_barrier((profiles, jac_oth))
    odd = place % 2
    head, tail = profiles[:rim], profiles[pixels - rim :]
    pairs = [(i, i ^ 1) for i in range(swath)]
    between = [(i, (i + 1 if i % 2 else i - 1)) for i in range(1, swath - 1)]
    prof_near = lax.ppermute(jnp.where(odd == 1, head, tail), "swath", pairs)
    prof_next = lax.ppermute(jnp.where(odd == 1, tail, head), "swath", between)

    smooth_own = half_call(
        False,
        (profiles, prof_near, prof_next, obs_top, obs_bot, jac_own, observed),
        (rates_own, rows, shift),
    )
    return half_call(
        True,
        (profiles, prof_near, prof_next, obs_top, obs_bot, jac_oth, mid_oth, bnd_oth, smooth_own, factor_two),
        (rates_oth, rows, shift),
    )


def solution(mesh):
    in_specs = (
        P("swath", None),
        P("swath", None, None),
        P("swath", None),
        P(),
        P(None, None, "chan"),
        P("chan", "swath"),
        P(None, "chan"),
        P("chan", None),
    )
    out_specs = P("chan", "swath")
    two = mesh.shape["chan"] == 2 and mesh.shape["swath"] % 4 == 0
    on_device = on_device_two if two else on_device_plain
    return jax.shard_map(
        on_device, mesh=mesh, in_specs=in_specs, out_specs=out_specs, check_vma=False
    )
```

```python
import functools
import math

import jax
import jax.numpy as jnp
import numpy as np
from jax import lax
from jax.experimental import pallas as pl
from jax.experimental.pallas import tpu as pltpu
from jax.sharding import PartitionSpec as P

XTRACK = 128
NANG = 8
HALO = 3
OUT_BLOCK = 512
GATHER_LIMIT = 60 * 1024 * 1024
OWN_LIMIT = 60 * 1024 * 1024
LAST_LIMIT = 60 * 1024 * 1024
SEGMENTS = 4
AHEAD = 2


max_zenith = math.pi / 3.0


def extended_2(block, sides, width):
    for axis, dim in sides:
        count = lax.axis_size(axis)
        forward = [(i, i + 1) for i in range(count - 1)]
        backward = [(target, source) for source, target in forward]
        low = lax.ppermute(
            lax.slice_in_dim(block, block.shape[dim] - width, None, axis=dim), axis, forward
        )
        high = lax.ppermute(lax.slice_in_dim(block, 0, width, axis=dim), axis, backward)
        block = jnp.concatenate([low, block, high], axis=dim)
    return block


def diffuse_once(extended, along_rate, cross_rate):
    center = extended[:, 1:-1]
    along_sum = extended[:, 2:] + extended[:, :-2] - 2.0 * center
    side_pad = jnp.pad(center, ((0, 0), (0, 0), (1, 1)))
    cross_sum = side_pad[:, :, 2:] + side_pad[:, :, :-2] - 2.0 * center
    return center + along_rate * along_sum + cross_rate * cross_sum


def line_rims(smooth_field):
    return extended_2(smooth_field, (("swath", 1),), 1)


def slant_of(angle_index):
    zenith = angle_index.astype(jnp.float32) * (max_zenith / (NANG - 1))
    return 1.0 / jnp.cos(zenith) - 1.0


def on_device_plain(grid_profiles, send_lists, counts, angle_index, jacobian, observed, kappa, factor):
    slot_rows = send_lists[0]
    slots = slot_rows.shape[1]
    own_chan = observed.shape[0]
    pixel_count = observed.shape[1]
    line_count = pixel_count // XTRACK
    live_slot = jnp.arange(slots, dtype=jnp.int32)[None, :] < counts[0][:, None]
    zero_value = jnp.zeros((), grid_profiles.dtype)
    outgoing = jnp.where(live_slot[:, :, None], grid_profiles[slot_rows], zero_value)
    incoming = lax.all_to_all(outgoing, "swath", split_axis=0, concat_axis=0, tiled=True)
    pixel_profiles = incoming.reshape(pixel_count, grid_profiles.shape[1])
    model = jnp.einsum("mkc,pk->mcp", jacobian, pixel_profiles, preferred_element_type=jnp.float32)
    slant_path = slant_of(angle_index)
    model = model.reshape(3, own_chan, line_count, XTRACK)
    departure = observed.astype(jnp.float32).reshape(own_chan, line_count, XTRACK) - (
        model[0] + slant_path * model[1] + slant_path * slant_path * model[2]
    )
    along_rate = kappa[0][:, None, None]
    cross_rate = kappa[1][:, None, None]
    smooth_field = departure
    for sweep in range(3):
        smooth_field = diffuse_once(line_rims(smooth_field), along_rate, cross_rate)
    smoothed = smooth_field.reshape(own_chan, pixel_count).astype(jnp.bfloat16)
    return jnp.dot(
        factor,
        lax.all_gather(smoothed, "chan", axis=0, tiled=True),
        preferred_element_type=jnp.float32,
    )


def gather_kernel(lists_hbm, counts_hbm, grid_hbm, out_hbm, lists, counts, grid, out, sems, out_sem):
    ins = [(lists_hbm, lists), (counts_hbm, counts), (grid_hbm, grid)]
    ins = [pltpu.make_async_copy(src, dst, sems.at[n]) for n, (src, dst) in enumerate(ins)]
    for copy in ins:
        copy.start()
    for copy in ins[:2]:
        copy.wait()
    grid_rows = grid.shape[0]
    parts, slots = lists.shape
    slot_number = lax.broadcasted_iota(jnp.int32, (slots, parts), 0)
    picks = jnp.where(slot_number < counts[...], lists[...].T, -1)
    row_number = lax.broadcasted_iota(jnp.int32, (slots, grid_rows), 1)
    ins[2].wait()
    for part in range(parts):
        one_hot = (picks[:, part : part + 1] == row_number).astype(jnp.float32).astype(jnp.bfloat16)
        rows = jnp.dot(one_hot, grid[...], preferred_element_type=jnp.float32)
        out[part] = rows.astype(out.dtype)
        pltpu.make_async_copy(out.at[part], out_hbm.at[part], out_sem).start()
    pltpu.make_async_copy(out, out_hbm, out_sem).wait()


def gather_rows(grid_profiles, slot_rows, counts):
    parts, slots = slot_rows.shape
    shape = (parts, slots, grid_profiles.shape[1])
    return pl.pallas_call(
        gather_kernel,
        out_shape=jax.ShapeDtypeStruct(shape, grid_profiles.dtype),
        in_specs=[pl.BlockSpec(memory_space=pl.ANY)] * 3,
        out_specs=pl.BlockSpec(memory_space=pl.ANY),
        scratch_shapes=[
            pltpu.VMEM(slot_rows.shape, jnp.int32),
            pltpu.VMEM(counts.shape, jnp.int32),
            pltpu.VMEM(grid_profiles.shape, grid_profiles.dtype),
            pltpu.VMEM(shape, grid_profiles.dtype),
            pltpu.SemaphoreType.DMA((3,)),
            pltpu.SemaphoreType.DMA,
        ],
        compiler_params=pltpu.CompilerParams(vmem_limit_bytes=GATHER_LIMIT),
        name="pick_rows",
    )(slot_rows, counts, grid_profiles)


def half_kernel(last, *refs):
    prof_hbm, prof_near_hbm, prof_next_hbm, top_hbm, bot_hbm, jac_hbm = refs[:6]
    if last:
        mid_hbm, bnd_hbm, smooth_hbm, factor_hbm, rates_hbm, rows_hbm, shift_hbm = refs[6:13]
        out_hbm, *refs, out, factor_ref = refs[13:]
    else:
        obs_hbm, rates_hbm, rows_hbm, shift_hbm = refs[6:10]
        out_hbm, *refs = refs[10:]
    prof, obs, jac_ref, field, moved_a, moved_b, smooth, rates_ref, rows_ref, shift_ref, sems, out_sems = refs
    own, pixels = jac_hbm.shape[1], prof_hbm.shape[0]
    odd = lax.rem(lax.axis_index("swath"), 2)
    rim = prof_near_hbm.shape[0]
    lines = pixels // XTRACK
    wide = 2 * XTRACK
    full = pixels + 2 * rim
    total = full // XTRACK
    first = own if last else 0
    groups = own // 16

    blocks = full // wide
    cuts = [blocks * n // SEGMENTS for n in range(SEGMENTS + 1)]
    waits = []
    copies = []

    def fetch(src, dst):
        copy = pltpu.make_async_copy(src, dst, sems.at[len(copies)])
        copies.append(copy)
        waits[-1].append(copy)

    for n in range(SEGMENTS):
        waits.append([])
        if n == 0:
            fetch(jac_hbm, jac_ref)
            fetch(rows_hbm, rows_ref)
            fetch(rates_hbm, rates_ref)
            fetch(shift_hbm, shift_ref)
            for src, number in ((prof_near_hbm, 1 - odd), (prof_next_hbm, odd)):
                fetch(src, prof.at[pl.ds(pl.multiple_of(number * (rim + pixels), XTRACK), rim), :])
            fetch(top_hbm, obs.at[:, pl.ds(0, rim)])
        low = max(cuts[n] * wide - rim, 0)
        high = min(cuts[n + 1] * wide - rim, pixels)
        fetch(prof_hbm.at[pl.ds(low, high - low), :], prof.at[pl.ds(rim + low, high - low), :])
        if last:
            spans = [(bnd_hbm, 0, 0, rim), (mid_hbm, 0, rim, pixels - rim), (bnd_hbm, rim, pixels - rim, pixels)]
        else:
            spans = [(obs_hbm, 0, 0, pixels)]
        for src, origin, begin, end in spans:
            begin_n, end_n = max(begin, low), min(end, high)
            if begin_n < end_n:
                fetch(
                    src.at[:, pl.ds(origin + begin_n - begin, end_n - begin_n)],
                    obs.at[:, pl.ds(rim + begin_n, end_n - begin_n)],
                )
        if n == SEGMENTS - 1:
            fetch(bot_hbm, obs.at[:, pl.ds(rim + pixels, rim)])
    if last:
        waits.append([])
        fetch(smooth_hbm, smooth.at[pl.ds(0, own), :])
        fetch(factor_hbm, factor_ref)

    def start(n):
        for copy in waits[n] if n < len(waits) else []:
            copy.start()

    for n in range(AHEAD):
        start(n)
    for copy in waits[0]:
        copy.wait()
    s1 = jnp.concatenate([rows_ref[0:1, :]] * 2, axis=1)
    s2 = jnp.concatenate([rows_ref[1:2, :]] * 2, axis=1)
    inside_top = rows_ref[2:3, :]
    inside_bot = rows_ref[3:4, :]

    def departures(t):
        at = pl.multiple_of(t * wide, wide)
        here = prof[pl.ds(at, wide), :]
        terms = [
            lax.dot_general(jac_ref[m], here, (((1,), (1,)), ((), ())), preferred_element_type=jnp.float32)
            for m in range(3)
        ]
        field[:, pl.ds(at, wide)] = obs[:, pl.ds(at, wide)].astype(jnp.float32) - (
            terms[0] + s1 * terms[1] + s2 * terms[2]
        )

    def shifts(i, moved):
        rows = pl.ds(pl.multiple_of(i * 16, 16), 16)
        tiles = []
        for j in range(1, total - 1):
            here = field[rows, j * XTRACK : (j + 1) * XTRACK]
            high = here.astype(jnp.bfloat16)
            low = (here - high.astype(jnp.float32)).astype(jnp.bfloat16)
            tiles.append(jnp.concatenate([high, low], axis=1))
        moved[...] = jnp.dot(
            jnp.concatenate(tiles, axis=0), shift_ref[...], preferred_element_type=jnp.float32
        )

    def sweeps(i, moved):
        rows = pl.ds(pl.multiple_of(i * 16, 16), 16)
        chan = pl.ds(pl.multiple_of(first + i * 16, 16), 16)
        along = jnp.broadcast_to(rates_ref[rows, 0:1], (16, XTRACK))
        cross = jnp.broadcast_to(rates_ref[rows, 1:2], (16, XTRACK))
        stay = 1.0 - 2.0 * along - 2.0 * cross
        along, cross = along / stay, cross / stay
        cross = [3.0 * cross, 3.0 * cross * cross, cross * cross * cross]
        stay = stay * stay * stay
        fields = [{}, {}, {}, {}]
        for j in range(total):
            fields[0][j] = field[rows, j * XTRACK : (j + 1) * XTRACK]
            for k in range(1, HALO + 1):
                at = j - k
                if at < k:
                    continue
                prev = fields[k - 1]
                new = (
                    prev[at]
                    + along * (prev[at - 1] + prev[at + 1])
                    + cross[k - 1] * moved[(at - 1) * 16 : at * 16, (k - 1) * XTRACK : k * XTRACK]
                )
                if at < HALO:
                    new = new * inside_top
                if at >= HALO + lines:
                    new = new * inside_bot
                fields[k][at] = new
                del prev[at - 1]
                if k == HALO:
                    line = at - HALO
                    smooth[chan, line * XTRACK : (line + 1) * XTRACK] = (new * stay).astype(smooth.dtype)

    for n in range(SEGMENTS):
        for copy in waits[n] if n else []:
            copy.wait()
        start(n + AHEAD)
        pl.loop(cuts[n], cuts[n + 1], unroll=cuts[n + 1] - cuts[n])(departures)

    def smooth_copy(n, size):
        rows = pl.ds(pl.multiple_of(n, 16), size)
        return pltpu.make_async_copy(smooth.at[rows, :], out_hbm.at[rows, :], out_sems.at[0])

    shifts(0, moved_a)

    @pl.loop(0, groups // 2, unroll=groups // 2)
    def _(h):
        shifts(2 * h + 1, moved_b)
        sweeps(2 * h, moved_a)
        shifts(jnp.minimum(2 * h + 2, groups - 1), moved_a)
        sweeps(2 * h + 1, moved_b)
        if not last:
            smooth_copy(32 * h, 32).start()

    if groups % 2:
        sweeps(groups - 1, moved_a)
        if not last:
            smooth_copy(16 * (groups - 1), 16).start()

    if not last:
        smooth_copy(0, own).wait()
        return

    for copy in waits[SEGMENTS]:
        copy.wait()

    def out_copy(t):
        at = pl.multiple_of(t * OUT_BLOCK, OUT_BLOCK)
        return pltpu.make_async_copy(
            out.at[:, pl.ds(at, OUT_BLOCK)], out_hbm.at[:, pl.ds(at, OUT_BLOCK)], out_sems.at[t]
        )

    @pl.loop(0, pixels // OUT_BLOCK, unroll=pixels // OUT_BLOCK)
    def _(t):
        at = pl.multiple_of(t * OUT_BLOCK, OUT_BLOCK)
        out[:, pl.ds(at, OUT_BLOCK)] = jnp.dot(
            factor_ref[...], smooth[:, pl.ds(at, OUT_BLOCK)], preferred_element_type=jnp.float32
        )
        out_copy(t).start()

    pl.loop(0, pixels // OUT_BLOCK)(lambda t: out_copy(t).wait())


def half_call(last, anys, small):
    own, pixels = anys[5].shape[1], anys[0].shape[0]
    rim = anys[1].shape[0]
    full = pixels + 2 * rim
    dtype = jnp.float32 if last else jnp.bfloat16
    scratch = [
        pltpu.VMEM((full, anys[0].shape[1]), jnp.bfloat16),
        pltpu.VMEM((own, full), jnp.bfloat16),
        pltpu.VMEM(anys[5].shape, jnp.bfloat16),
        pltpu.VMEM((own, full), jnp.float32),
        pltpu.VMEM((16 * (full // XTRACK - 2), HALO * XTRACK), jnp.float32),
        pltpu.VMEM((16 * (full // XTRACK - 2), HALO * XTRACK), jnp.float32),
        pltpu.VMEM((2 * own if last else own, pixels), jnp.bfloat16),
        *[pltpu.VMEM(x.shape, x.dtype) for x in small],
        pltpu.SemaphoreType.DMA((32,)),
        pltpu.SemaphoreType.DMA((pixels // OUT_BLOCK,)),
    ]
    if last:
        scratch += [pltpu.VMEM((own, pixels), jnp.float32), pltpu.VMEM((own, 2 * own), jnp.bfloat16)]
    return pl.pallas_call(
        functools.partial(half_kernel, last),
        out_shape=jax.ShapeDtypeStruct((own, pixels), dtype),
        in_specs=[pl.BlockSpec(memory_space=pl.ANY)] * (len(anys) + len(small)),
        out_specs=pl.BlockSpec(memory_space=pl.ANY),
        scratch_shapes=scratch,
        compiler_params=pltpu.CompilerParams(vmem_limit_bytes=LAST_LIMIT if last else OWN_LIMIT),
        name="other_half_and_factor" if last else "own_half",
    )(*anys, *small)


def on_device_two(grid_profiles, send_lists, counts, angle_index, jacobian, observed, kappa, factor):
    own, pixels = observed.shape
    rim = HALO * XTRACK
    swath = lax.axis_size("swath")
    place = lax.axis_index("swath")
    half = lax.axis_index("chan")
    swap = [(0, 1), (1, 0)]
    forward = [(i, i + 1) for i in range(swath - 1)]
    backward = [(i + 1, i) for i in range(swath - 1)]

    jac_own = jnp.swapaxes(jacobian, 1, 2)
    quarter = own // 4
    jac_part = lax.dynamic_slice_in_dim(jac_own, (place % 4) * quarter, quarter, axis=1)
    jac_near = lax.ppermute(jac_part, "chan", swap)
    rates_own = kappa.T
    rates_oth = lax.ppermute(rates_own, "chan", swap)
    outgoing = gather_rows(grid_profiles, send_lists[0], counts)
    outgoing, obs_late = lax.optimization_barrier((outgoing, observed))
    bnd_own = jnp.concatenate([obs_late[:, :rim], obs_late[:, pixels - rim :]], axis=1)
    bnd_oth = lax.ppermute(bnd_own, "chan", swap)
    own_rims = [lax.ppermute(bnd_own[:, rim:], "swath", forward), lax.ppermute(bnd_own[:, :rim], "swath", backward)]
    incoming = lax.all_to_all(outgoing, "swath", split_axis=0, concat_axis=0, tiled=True)
    middle = obs_late[:, rim : pixels - rim]
    middle, bnd_oth, jac_near = lax.optimization_barrier((middle, bnd_oth, jac_near))
    mid_oth = lax.ppermute(middle, "chan", swap)
    jac_oth = jac_near
    for step in (1, 2):
        jac_far = lax.ppermute(jac_oth, "swath", [(i, i ^ step) for i in range(swath)])
        jac_oth = jnp.where(
            place // step % 2 == 0,
            jnp.concatenate([jac_oth, jac_far], axis=1),
            jnp.concatenate([jac_far, jac_oth], axis=1),
        )
    near = np.eye(XTRACK, k=1) + np.eye(XTRACK, k=-1)
    moves = np.concatenate([near, near @ near, near @ near @ near], axis=1)
    shift = jnp.asarray(np.concatenate([moves, moves], axis=0), jnp.bfloat16)
    slant = slant_of(angle_index)
    ones = jnp.ones((XTRACK,), jnp.float32)
    rows = jnp.stack([
        slant,
        slant * slant,
        jnp.where(place > 0, ones, 0.0),
        jnp.where(place < swath - 1, ones, 0.0),
    ])
    factor_two = jnp.where(half == 0, factor, jnp.roll(factor, own, axis=1))

    bnd_oth, rates_oth, rows, factor_two = lax.optimization_barrier(
        (bnd_oth, rates_oth, rows, factor_two)
    )
    oth_rims = [lax.ppermute(bnd_oth[:, rim:], "swath", forward), lax.ppermute(bnd_oth[:, :rim], "swath", backward)]

    profiles = incoming.reshape(pixels, grid_profiles.shape[1])
    profiles, jac_oth = lax.optimization_barrier((profiles, jac_oth))
    odd = place % 2
    head, tail = profiles[:rim], profiles[pixels - rim :]
    pairs = [(i, i ^ 1) for i in range(swath)]
    between = [(i, (i + 1 if i % 2 else i - 1)) for i in range(1, swath - 1)]
    prof_near = lax.ppermute(jnp.where(odd == 1, head, tail), "swath", pairs)
    prof_next = lax.ppermute(jnp.where(odd == 1, tail, head), "swath", between)

    smooth_own = half_call(
        False,
        (profiles, prof_near, prof_next, *own_rims, jac_own, observed),
        (rates_own, rows, shift),
    )
    return half_call(
        True,
        (profiles, prof_near, prof_next, *oth_rims, jac_oth, mid_oth, bnd_oth, smooth_own, factor_two),
        (rates_oth, rows, shift),
    )


def solution(mesh):
    in_specs = (
        P("swath", None),
        P("swath", None, None),
        P("swath", None),
        P(),
        P(None, None, "chan"),
        P("chan", "swath"),
        P(None, "chan"),
        P("chan", None),
    )
    out_specs = P("chan", "swath")
    two = mesh.shape["chan"] == 2 and mesh.shape["swath"] % 4 == 0
    on_device = on_device_two if two else on_device_plain
    return jax.shard_map(
        on_device, mesh=mesh, in_specs=in_specs, out_specs=out_specs, check_vma=False
    )
```
